32 devices in a mesh: groups: 2 (over x), ao: 16 (over z, y, core).
Axes of the slice: x: 2, y: 2, z: 4, core: 2. Of those that a mesh axis runs over, the one named last changes fastest.
Arguments:
- tiles: bfloat16 [64, 128, 128, 128], P('ao', None, 'groups'), parts along dimension 2, may hold values from -6 to 6
- pairs: int32 [64, 2], replicated, may hold values from 0 to 63, as said below
- occ_coef: bfloat16 [6144, 8], replicated, may hold values from -0.3125 to 0.3125
- vir_coef: bfloat16 [6144, 4864], P(None, 'ao'), may hold values from -0.078125 to 0.078125
Outputs:
- pair_ints: bfloat16 [4864, 1024], P('ao', 'groups'), parts along dimension 1
The draws below stay inside these ranges and needn't reach their ends.
There are 2 independent parts, one for each index of `groups`. The reference program is written for one: setup_inputs(seed, part) draws one part's arguments, and reference() takes and returns one part's arrays. A program takes and returns all parts, laid end to end along the dimension named above; an argument that names none is the same for every part. Nothing has to cross between parts.
Inputs may be any that keep to these rules, and one draw needn't show every extreme that they name: `pairs`: device d of ao holds tiles d * 4 to (d + 1) * 4 - 1. The column groups of one device's tiles are 4 consecutive groups (modulo 64); the row group of a tile differs from its column group by at most 3, cyclically.
All inputs are finite; a program needn't handle non-finite values.
Results may differ from the reference program's by a relative error of at most 0.0056.
Values may be sent and summed in bfloat16 or wider, within the bound.
No kernel may reach another device: no remote copies, remote signals or barrier semaphores. Data moves between devices by JAX's collectives and lax.ppermute only.
A program may use at most 128 MiB of HBM per device.

```python
import jax
import jax.numpy as jnp
from jax import lax

NGROUP = 64
AO_GROUP = 96
TILE = 128
P_SIZE = 64
NVIR = 4864
OCC_B = 8
TILES_DEV = 4
NAO = 6144
NT = 64


def draw_pairs(key, part):
    key = jax.random.fold_in(key, 11)
    devices = NT // TILES_DEV
    owned = NGROUP // devices
    key_shift, key_first, key_offset = jax.random.split(key, 3)
    shifts = jax.random.randint(key_shift, (devices,), 0, NGROUP)
    aligned = owned * jax.random.randint(key_first, (), 0, NGROUP // owned)
    shifts = shifts.at[0].set(aligned)
    slots = jnp.arange(TILES_DEV)
    columns = (shifts[:, None] + slots[None, :]) % NGROUP
    offsets = jax.random.randint(key_offset, (devices, TILES_DEV), -3, 4)
    row_groups = (columns + offsets) % NGROUP
    return jnp.stack([row_groups.reshape(-1), columns.reshape(-1)], axis=1).astype(jnp.int32)


def level_of(rng, extent, shards, least, largest):
    gain = 1.0
    for dim, parts in shards:
        draws = jax.random.uniform(jax.random.fold_in(jax.random.fold_in(rng, 6), dim), (parts,), jnp.float32, least / len(shards), largest / len(shards))
        gain = gain * jnp.repeat(jnp.exp(draws), extent[dim] // parts).reshape((-1,) + (1,) * (len(extent) - 1 - dim))
    return gain


def noise(key, shape, scale, reach, cuts=(), kind=jnp.bfloat16):
    array = jax.random.normal(key, shape, jnp.float32) * scale
    if len(cuts) > 0:
        array = level_of(key, shape, cuts, -0.22, 0.18) * array
    return jnp.clip(array, min=-reach, max=reach).astype(kind)


def setup_inputs(seed: int = 0, part: int = 0) -> dict:
    arg_keys = jax.random.split(jax.random.key(seed), 5)
    own_keys = jax.random.split(jax.random.fold_in(arg_keys[4], part), 5)
    return {
        "tiles": noise(own_keys[0], (NT, TILE, P_SIZE, TILE), 1.0, 6.0, ((0, 16),)),
        "pairs": draw_pairs(jax.random.fold_in(arg_keys[4], 71), part),
        "occ_coef": noise(arg_keys[2], (NAO, OCC_B), (4 * AO_GROUP) ** -0.5, 0.3125),
        "vir_coef": noise(arg_keys[3], (NAO, NVIR), NAO ** -0.5, 0.078125, ((1, 16),)),
    }


def reference(tiles, pairs, occ_coef, vir_coef):
    groups = occ_coef.reshape(NGROUP, AO_GROUP, OCC_B).astype(jnp.float32)

    def add_tile(accumulated, scan_item):
        tile_block, tile_pair = scan_item
        coef_rows = lax.dynamic_index_in_dim(groups, tile_pair[0].astype(jnp.int32), 0, keepdims=False)
        used_block = tile_block[:AO_GROUP, :, :AO_GROUP].astype(jnp.float32)
        half_ints = jnp.einsum("ri,rqc->ciq", coef_rows, used_block).reshape(AO_GROUP, OCC_B * P_SIZE)
        rounded = lax.optimization_barrier(half_ints.astype(jnp.bfloat16))
        accumulated = accumulated.at[tile_pair[1]].add(rounded.astype(jnp.float32))
        return accumulated, None

    start_sum = jnp.zeros((NGROUP, AO_GROUP, OCC_B * P_SIZE), jnp.float32)
    summed, unused = lax.scan(add_tile, start_sum, (tiles, pairs))
    half_x = summed.reshape(NAO, OCC_B * P_SIZE).astype(jnp.bfloat16)
    result = lax.dot_general(vir_coef, half_x, (((0,), (0,)), ((), ())), preferred_element_type=jnp.float32)
    return result.astype(jnp.bfloat16)
```

```python
import functools

import jax
import jax.numpy as jnp
from jax import lax
from jax.experimental import pallas as pl
from jax.experimental.pallas import tpu as pltpu
from jax.sharding import PartitionSpec as P

NGROUP = 64
AO_GROUP = 96
LANES = 128
QB = 16
CHUNKS = 2
VMEM_LIMIT = 48 * 1024 * 1024


def first_group(pairs, dev, count):
    cols = [pairs[1, dev * count + j] for j in range(count)]
    first = cols[0]
    for col in cols[1:]:
        before = lax.rem(col + (NGROUP - 1), NGROUP)
        is_first = functools.reduce(jnp.logical_and, [other != before for other in cols])
        first = jnp.where(is_first, col, first)
    before = lax.rem(cols[0] + (NGROUP - 1), NGROUP)
    is_first = functools.reduce(jnp.logical_and, [other != before for other in cols])
    return jnp.where(is_first, cols[0], first)


def tile_of_slot(pairs, dev, count, slot):
    wanted = lax.rem(first_group(pairs, dev, count) + slot, NGROUP)
    found = jnp.int32(0)
    for j in range(1, count):
        found = jnp.where(pairs[1, dev * count + j] == wanted, j, found)
    return found


def half_kernel(count, occ_batch, pairs, me, occ_ref, tile_ref, out_ref, spread, held):
    slot = pl.program_id(0)
    width = AO_GROUP * QB
    q_chunk = tile_ref.shape[2]

    @pl.when(slot == 0)
    def _():
        row = lax.broadcasted_iota(jnp.int32, (LANES, width), 0)
        lane = lax.broadcasted_iota(jnp.int32, (LANES, width), 1)
        spread[...] = (lane // QB == row).astype(jnp.bfloat16)

    tile = tile_of_slot(pairs, me[0], count, slot)
    offset = pairs[0, me[0] * count + tile] * AO_GROUP
    start = pl.multiple_of(offset // LANES * LANES, LANES)
    last = occ_ref.shape[1] - LANES
    after = pl.multiple_of(jnp.minimum(start + LANES, last), LANES)
    shift = offset - start
    low = occ_ref[:, pl.ds(start, LANES)].astype(jnp.float32)
    high = occ_ref[:, pl.ds(after, LANES)].astype(jnp.float32)
    turn = lax.rem(LANES - shift, LANES)
    low, high = pltpu.roll(low, turn, 1), pltpu.roll(high, turn, 1)
    lane = lax.broadcasted_iota(jnp.int32, low.shape, 1)
    coef = jnp.where(lane < LANES - shift, low, high).astype(jnp.bfloat16)
    wide = jnp.dot(coef, spread[...], preferred_element_type=jnp.float32)
    wide = jnp.broadcast_to(wide[:, None, :], (occ_batch, QB, width))
    q_row = lax.broadcasted_iota(jnp.int32, wide.shape, 1)
    q_col = lax.broadcasted_iota(jnp.int32, wide.shape, 2) % QB
    kron = jnp.where(q_row == q_col, wide, 0.0).reshape(occ_batch * QB, width).astype(jnp.bfloat16)
    for block in range(q_chunk // QB):
        part = tile_ref[0, :, block * QB : (block + 1) * QB, :].reshape(width, LANES)
        half = jnp.dot(kron, part, preferred_element_type=jnp.float32)
        held[slot, :, block * QB : (block + 1) * QB, :] = half.reshape(occ_batch, QB, LANES)

    @pl.when(slot == count - 1)
    def _():
        rows = occ_batch * q_chunk
        lane = lax.broadcasted_iota(jnp.int32, (rows, LANES), 1)
        pieces = [held[s].reshape(rows, LANES) for s in range(count)]
        for out in range(count * AO_GROUP // LANES):
            value = None
            for s in range(count):
                begin, end = s * AO_GROUP - out * LANES, (s + 1) * AO_GROUP - out * LANES
                if end <= 0 or begin >= LANES:
                    continue
                turned = pieces[s] if begin % LANES == 0 else pltpu.roll(pieces[s], begin % LANES, 1)
                value = turned if value is None else jnp.where(lane < begin, value, turned)
            out_ref[:, out * LANES : (out + 1) * LANES] = value.astype(out_ref.dtype)


def half_chunk(pairs, me, occ, tiles, chunk):
    count, ri_width = tiles.shape[0], tiles.shape[2]
    occ_batch = occ.shape[0]
    q_chunk = ri_width // CHUNKS
    rows, columns = occ_batch * q_chunk, count * AO_GROUP
    return pl.pallas_call(
        functools.partial(half_kernel, count, occ_batch),
        grid_spec=pltpu.PrefetchScalarGridSpec(
            num_scalar_prefetch=2,
            grid=(count,),
            in_specs=[
                pl.BlockSpec(occ.shape, lambda s, pairs, me: (0, 0)),
                pl.BlockSpec(
                    (1, AO_GROUP, q_chunk, LANES),
                    lambda s, pairs, me: (tile_of_slot(pairs, me[0], count, s), 0, chunk, 0),
                ),
            ],
            out_specs=pl.BlockSpec((rows, columns), lambda s, pairs, me: (0, 0)),
            scratch_shapes=[
                pltpu.VMEM((LANES, AO_GROUP * QB), jnp.bfloat16),
                pltpu.VMEM((count, occ_batch, q_chunk, LANES), jnp.float32),
            ],
        ),
        out_shape=jax.ShapeDtypeStruct((rows, columns), jnp.bfloat16),
        compiler_params=pltpu.CompilerParams(vmem_limit_bytes=VMEM_LIMIT),
        cost_estimate=pl.CostEstimate(
            flops=2 * rows * columns * AO_GROUP * QB, bytes_accessed=tiles.size, transcendentals=0
        ),
        name="half_transform",
    )(pairs, me, occ, tiles)


def chip_of(place, chips):
    return jnp.where(place < chips // 2, 2 * place, 2 * (chips - 1 - place) + 1)


def place_of(chip, chips):
    return jnp.where(lax.rem(chip, 2) == 0, chip // 2, chips - 1 - chip // 2)


def source_chip(chip, step, chips):
    away = (step + 1) // 2
    away = jnp.where(lax.rem(step, 2) == 1, chips - away, away)
    return chip_of(lax.rem(place_of(chip, chips) + away, chips), chips)


def window_kernel(count, chips, pairs, me, vir_ref, own_ref, other_ref):
    step = pl.program_id(0)
    chip, core = me[0] // 2, lax.rem(me[0], 2)
    source = source_chip(chip, step, chips)
    tiles_all = vir_ref.shape[1] // LANES
    for dev, out_ref in ((2 * source + core, own_ref), (2 * source + 1 - core, other_ref)):
        offset = first_group(pairs, dev, count) * AO_GROUP
        start = offset // LANES
        shift = offset - start * LANES
        turn = lax.rem(LANES - shift, LANES)
        lane = lax.broadcasted_iota(jnp.int32, (vir_ref.shape[0], LANES), 1)
        before = None
        for j in range(count * AO_GROUP // LANES + 1):
            at = pl.multiple_of(lax.rem(start + j, tiles_all) * LANES, LANES)
            turned = pltpu.roll(vir_ref[:, pl.ds(at, LANES)].astype(jnp.float32), turn, 1)
            if before is not None:
                value = jnp.where(lane < LANES - shift, before, turned)
                out_ref[:, (j - 1) * LANES : j * LANES] = value.astype(out_ref.dtype)
            before = turned


def windows(pairs, me, vir, count, chips):
    rows, columns = vir.shape[0], count * AO_GROUP
    shape = jax.ShapeDtypeStruct((rows, chips * columns), vir.dtype)
    spec = pl.BlockSpec((rows, columns), lambda k, pairs, me: (0, k))
    return pl.pallas_call(
        functools.partial(window_kernel, count, chips),
        grid_spec=pltpu.PrefetchScalarGridSpec(
            num_scalar_prefetch=2,
            grid=(chips,),
            in_specs=[pl.BlockSpec(vir.shape, lambda k, pairs, me: (0, 0))],
            out_specs=[spec, spec],
        ),
        out_shape=[shape, shape],
        compiler_params=pltpu.CompilerParams(vmem_limit_bytes=VMEM_LIMIT),
        cost_estimate=pl.CostEstimate(flops=0, bytes_accessed=6 * vir.size, transcendentals=0),
        name="vir_windows",
    )(pairs, me, vir)


def join_kernel(occ_batch, *refs):
    out_ref = refs[-1]
    sums = [refs[c][...] + refs[CHUNKS + c][...] for c in range(CHUNKS)]
    q_chunk = sums[0].shape[1] // occ_batch
    rows = sums[0].shape[0]
    lane = lax.broadcasted_iota(jnp.int32, (rows, LANES), 1)
    per_tile = LANES // q_chunk
    for out in range(out_ref.shape[1] // LANES):
        value = None
        for piece in range(per_tile):
            i, c = divmod(out * per_tile + piece, CHUNKS)
            tile, at = divmod(i * q_chunk, LANES)
            part = sums[c][:, tile * LANES : (tile + 1) * LANES]
            turn = (piece * q_chunk - at) % LANES
            part = part if turn == 0 else pltpu.roll(part, turn, 1)
            value = part if value is None else jnp.where(lane < piece * q_chunk, value, part)
        out_ref[:, out * LANES : (out + 1) * LANES] = value.astype(out_ref.dtype)


def join(own, received, occ_batch):
    rows, columns = own[0].shape
    return pl.pallas_call(
        functools.partial(join_kernel, occ_batch),
        out_shape=jax.ShapeDtypeStruct((rows, CHUNKS * columns), jnp.bfloat16),
        compiler_params=pltpu.CompilerParams(vmem_limit_bytes=VMEM_LIMIT),
        name="join_cores",
    )(*own, *received)


def on_device(chips, tiles, pairs, occ_coef, vir_coef):
    count = tiles.shape[0]
    occ_batch = occ_coef.shape[1]
    columns = count * AO_GROUP
    me = lax.axis_index("ao").astype(jnp.int32).reshape(1)
    pairs, occ, vir = pairs.T, occ_coef.T, vir_coef.T

    ring = [2 * p if p < chips // 2 else 2 * (chips - 1 - p) + 1 for p in range(chips)]
    forward = [(2 * ring[p] + c, 2 * ring[(p + 1) % chips] + c) for p in range(chips) for c in (0, 1)]
    backward = [(b, a) for a, b in forward]
    across = [(d, d ^ 1) for d in range(2 * chips)]

    ahead = [half_chunk(pairs, me, occ, tiles, c) for c in range(CHUNKS)]
    behind = list(ahead)
    own_w, other_w = windows(pairs, me, vir, count, chips)
    other_w = lax.ppermute(other_w, "ao", across)

    sums = [[None, None] for _ in range(CHUNKS)]

    def use(c, step, block):
        for which, w in enumerate((own_w, other_w)):
            term = lax.dot_general(
                w[:, step * columns : (step + 1) * columns],
                block,
                (((1,), (1,)), ((), ())),
                preferred_element_type=jnp.float32,
            )
            sums[c][which] = term if sums[c][which] is None else sums[c][which] + term

    for c in range(CHUNKS):
        use(c, 0, ahead[c])
    for away in range(1, chips // 2):
        for c in range(CHUNKS):
            ahead[c] = lax.ppermute(ahead[c], "ao", forward)
            behind[c] = lax.ppermute(behind[c], "ao", backward)
        for c in range(CHUNKS):
            use(c, 2 * away - 1, ahead[c])
            use(c, 2 * away, behind[c])
    for c in range(CHUNKS):
        last = lax.ppermute(ahead[c], "ao", forward) if c < CHUNKS // 2 else lax.ppermute(behind[c], "ao", backward)
        use(c, chips - 1, last)

    received = [lax.ppermute(sums[c][1], "ao", across) for c in range(CHUNKS)]
    return join([sums[c][0] for c in range(CHUNKS)], received, occ_batch)


def solution(mesh):
    return jax.shard_map(
        functools.partial(on_device, mesh.shape["ao"] // 2),
        mesh=mesh,
        in_specs=(P("ao", None, "groups", None), P(), P(), P(None, "ao")),
        out_specs=P("ao", "groups"),
        check_vma=False,
    )
```

```python
import functools

import jax
import jax.numpy as jnp
from jax import lax
from jax.experimental import pallas as pl
from jax.experimental.pallas import tpu as pltpu
from jax.sharding import PartitionSpec as P

NGROUP = 64
AO_GROUP = 96
LANES = 128
QB = 16
PAIR = 2
VMEM_LIMIT = 56 * 1024 * 1024


def occupied_rows(occ_ref, offset):
    start = pl.multiple_of((offset // LANES) * LANES, LANES)
    after = pl.multiple_of(jnp.minimum(start + LANES, occ_ref.shape[1] - LANES), LANES)
    shift = offset - start
    turn = lax.rem(LANES - shift, LANES)
    low = pltpu.roll(occ_ref[:, pl.ds(start, LANES)].astype(jnp.float32), turn, 1)
    high = pltpu.roll(occ_ref[:, pl.ds(after, LANES)].astype(jnp.float32), turn, 1)
    lane = lax.broadcasted_iota(jnp.int32, low.shape, 1)
    return jnp.where(lane < LANES - shift, low, high)


def half_kernel(me, pairs_hbm, occ_hbm, tiles_ref, out_ref, pairs, occ, held_tiles, kron, held, sems):
    count, ri_width = tiles_ref.shape[0], tiles_ref.shape[2]
    occ_batch = occ_hbm.shape[0]
    width = AO_GROUP * QB
    pairs_copy = pltpu.make_async_copy(pairs_hbm, pairs, sems.at[count])
    occ_copy = pltpu.make_async_copy(occ_hbm, occ, sems.at[count + 1])
    pairs_copy.start()
    occ_copy.start()
    copies = [
        pltpu.make_async_copy(tiles_ref.at[t, pl.ds(0, AO_GROUP)], held_tiles.at[t], sems.at[t]) for t in range(count)
    ]
    for copy in copies:
        copy.start()
    row = lax.broadcasted_iota(jnp.int32, (LANES, width), 0)
    lane = lax.broadcasted_iota(jnp.int32, (LANES, width), 1)
    spread = jnp.where(jnp.right_shift(lane, QB.bit_length() - 1) == row, 1.0, 0.0).astype(jnp.bfloat16)
    q_row = lax.broadcasted_iota(jnp.int32, (QB, width), 0)
    q_col = jnp.bitwise_and(lax.broadcasted_iota(jnp.int32, (QB, width), 1), QB - 1)
    diagonal = q_row == q_col
    pairs_copy.wait()
    occ_copy.wait()
    first = me[0] * count
    coef = [occupied_rows(occ, pairs[0, first + t] * AO_GROUP) for t in range(count)]
    coef = jnp.concatenate(coef, 0).astype(jnp.bfloat16)
    wide = jnp.dot(coef, spread, preferred_element_type=jnp.float32)
    for t in range(count):
        for i in range(occ_batch):
            rows = jnp.broadcast_to(wide[t * occ_batch + i : t * occ_batch + i + 1], (QB, width))
            kron[t, i * QB : (i + 1) * QB, :] = jnp.where(diagonal, rows, 0.0).astype(jnp.bfloat16)
    for t in range(count):
        copies[t].wait()
        for b in range(0, ri_width // QB, PAIR):
            parts = [held_tiles[t, :, (b + k) * QB : (b + k + 1) * QB, :].reshape(width, LANES) for k in range(PAIR)]
            half = jnp.dot(kron[t], jnp.concatenate(parts, 1), preferred_element_type=jnp.float32)
            for k in range(PAIR):
                part = half[:, k * LANES : (k + 1) * LANES].reshape(occ_batch, QB, LANES)
                held[t, :, (b + k) * QB : (b + k + 1) * QB, :] = part
    rows = occ_batch * ri_width
    lane = lax.broadcasted_iota(jnp.int32, (rows, LANES), 1)
    pieces = []
    for s in range(count):
        tile = jnp.int32(0)
        for j in range(1, count):
            tile = jnp.where(lax.rem(pairs[1, first + j], count) == s, j, tile)
        pieces.append(held[tile].reshape(rows, LANES))
    for out in range(count * AO_GROUP // LANES):
        value = None
        for s in range(count):
            begin, end = s * AO_GROUP - out * LANES, (s + 1) * AO_GROUP - out * LANES
            if end <= 0 or begin >= LANES:
                continue
            turned = pieces[s] if begin % LANES == 0 else pltpu.roll(pieces[s], begin % LANES, 1)
            value = turned if value is None else jnp.where(lane < begin, value, turned)
        out_ref[:, out * LANES : (out + 1) * LANES] = value.astype(out_ref.dtype)


def half_transform(me, pairs, occ, tiles):
    count, ri_width = tiles.shape[0], tiles.shape[2]
    occ_batch = occ.shape[0]
    width = AO_GROUP * QB
    rows, columns = occ_batch * ri_width, count * AO_GROUP
    return pl.pallas_call(
        half_kernel,
        in_specs=[pl.BlockSpec(memory_space=pltpu.SMEM)] + [pl.BlockSpec(memory_space=pl.ANY)] * 3,
        out_specs=pl.BlockSpec(memory_space=pltpu.VMEM),
        out_shape=jax.ShapeDtypeStruct((rows, columns), jnp.bfloat16),
        scratch_shapes=[
            pltpu.SMEM(pairs.shape, jnp.int32),
            pltpu.VMEM(occ.shape, jnp.bfloat16),
            pltpu.VMEM((count, AO_GROUP, ri_width, LANES), jnp.bfloat16),
            pltpu.VMEM((count, occ_batch * QB, width), jnp.bfloat16),
            pltpu.VMEM((count, occ_batch, ri_width, LANES), jnp.float32),
            pltpu.SemaphoreType.DMA((count + 2,)),
        ],
        compiler_params=pltpu.CompilerParams(vmem_limit_bytes=VMEM_LIMIT),
        cost_estimate=pl.CostEstimate(
            flops=2 * rows * columns * width, bytes_accessed=2 * tiles.size, transcendentals=0
        ),
        name="half_transform",
    )(me, pairs, occ, tiles)


def chip_at(place, chips):
    place = lax.rem(place + chips, chips)
    return jnp.where(place < chips // 2, 2 * place, 2 * (chips - 1 - place) + 1)


def place_of(chip, chips):
    return jnp.where(lax.rem(chip, 2) == 0, chip // 2, chips - 1 - chip // 2)


def take_windows(count, pairs, vir_ref, dev, write):
    columns = count * AO_GROUP
    panels = vir_ref.shape[1] // columns
    cols = [pairs[1, dev * count + j] for j in range(count)]
    first = cols[0]
    for col in cols:
        before = lax.rem(col + (NGROUP - 1), NGROUP)
        is_first = functools.reduce(jnp.logical_and, [other != before for other in cols])
        first = jnp.where(is_first, col, first)
    panel = first // count
    bound = lax.rem(first, count) * AO_GROUP
    low = pl.multiple_of(panel * columns, LANES)
    high = pl.multiple_of(lax.rem(panel + 1, panels) * columns, LANES)
    for j in range(columns // LANES):
        lane = lax.broadcasted_iota(jnp.int32, (vir_ref.shape[0], LANES), 1) + j * LANES
        here = vir_ref[:, pl.ds(pl.multiple_of(low + j * LANES, LANES), LANES)]
        there = vir_ref[:, pl.ds(pl.multiple_of(high + j * LANES, LANES), LANES)]
        write(j, jnp.where(lane >= bound, here, there))


def window_kernel(count, chips, me, pairs, own_ref, other_ref, both_ref, last_ref):
    chip, core = me[0] // 2, lax.rem(me[0], 2)
    place = place_of(chip, chips)
    behind = 2 * core - 1
    rows, columns = own_ref.shape[0], count * AO_GROUP
    for k in range(chips - 1):
        source = chip_at(place + behind * ((k + 1) // 2), chips)
        dev = 2 * source + (core if k == 0 or k % 2 == 1 else 1 - core)
        for half, vir_ref in enumerate((own_ref, other_ref)):

            def write(j, value, k=k, half=half):
                at = k * columns + j * LANES
                both_ref[half * rows : (half + 1) * rows, at : at + LANES] = value

            take_windows(count, pairs, vir_ref, dev, write)
    source = chip_at(place + chips // 2, chips)
    for k, dev in enumerate((2 * source + core, 2 * source + 1 - core)):

        def write(j, value, k=k):
            at = k * columns + j * LANES
            last_ref[:, at : at + LANES] = value

        take_windows(count, pairs, own_ref, dev, write)


def windows(me, pairs, vir, other_vir, count, chips):
    rows, columns = vir.shape[0], count * AO_GROUP
    smem, vmem = pl.BlockSpec(memory_space=pltpu.SMEM), pl.BlockSpec(memory_space=pltpu.VMEM)
    return pl.pallas_call(
        functools.partial(window_kernel, count, chips),
        in_specs=[smem, smem, vmem, vmem],
        out_specs=[vmem, vmem],
        out_shape=[
            jax.ShapeDtypeStruct((2 * rows, (chips - 1) * columns), vir.dtype),
            jax.ShapeDtypeStruct((rows, 2 * columns), vir.dtype),
        ],
        compiler_params=pltpu.CompilerParams(vmem_limit_bytes=VMEM_LIMIT),
        cost_estimate=pl.CostEstimate(flops=0, bytes_accessed=8 * vir.size, transcendentals=0),
        name="vir_windows",
    )(me, pairs, vir, other_vir)


def product(vir, block):
    return lax.dot_general(vir, block, (((1,), (1,)), ((), ())), preferred_element_type=jnp.float32)


def on_device(chips, tiles, pairs, occ_coef, vir_coef):
    count = tiles.shape[0]
    columns = count * AO_GROUP
    me = lax.axis_index("ao").astype(jnp.int32).reshape(1)
    pairs, occ, vir = pairs.T, occ_coef.T, vir_coef.T
    rows = vir.shape[0]

    ring = [2 * p if p < chips // 2 else 2 * (chips - 1 - p) + 1 for p in range(chips)]
    links = [(ring[p], ring[(p + 1) % chips]) for p in range(chips)]
    onward = [(2 * a, 2 * b) for a, b in links] + [(2 * b + 1, 2 * a + 1) for a, b in links]
    across = [(d, d ^ 1) for d in range(2 * chips)]

    own = half_transform(me, pairs, occ, tiles)
    both_w, last_w = windows(me, pairs, vir, lax.ppermute(vir, "ao", across), count, chips)
    travelling = [own, lax.ppermute(own, "ao", across)]
    sums = product(both_w[:, :columns], own)
    for hop in range(1, chips // 2):
        for which in range(2):
            travelling[which] = lax.ppermute(travelling[which], "ao", onward)
            k = 2 * hop - 1 + which
            sums = sums + product(both_w[:, k * columns : (k + 1) * columns], travelling[which])
    received = lax.ppermute(sums[rows:], "ao", across)
    last = lax.ppermute(travelling[0], "ao", onward)
    total = sums[:rows] + received + product(last_w[:, :columns], last)
    total = total + product(last_w[:, columns:], lax.ppermute(last, "ao", across))
    return total.astype(jnp.bfloat16)


def solution(mesh):
    return jax.shard_map(
        functools.partial(on_device, mesh.shape["ao"] // 2),
        mesh=mesh,
        in_specs=(P("ao", None, "groups", None), P(), P(), P(None, "ao")),
        out_specs=P("ao", "groups"),
        check_vma=False,
    )
```

```python
import functools

import jax
import jax.numpy as jnp
from jax import lax
from jax.experimental import pallas as pl
from jax.experimental.pallas import tpu as pltpu
from jax.sharding import PartitionSpec as P

NGROUP = 64
AO_GROUP = 96
LANES = 128
QB = 16
PAIR = 2
HALF_VMEM = 56 * 1024 * 1024
WINDOW_VMEM = 24 * 1024 * 1024


def occupied_rows(occ_ref, offset):
    start = pl.multiple_of((offset // LANES) * LANES, LANES)
    after = pl.multiple_of(jnp.minimum(start + LANES, occ_ref.shape[1] - LANES), LANES)
    shift = offset - start
    turn = lax.rem(LANES - shift, LANES)
    low = pltpu.roll(occ_ref[:, pl.ds(start, LANES)].astype(jnp.float32), turn, 1)
    high = pltpu.roll(occ_ref[:, pl.ds(after, LANES)].astype(jnp.float32), turn, 1)
    lane = lax.broadcasted_iota(jnp.int32, low.shape, 1)
    return jnp.where(lane < LANES - shift, low, high)


def half_kernel(me, pairs_hbm, occ_hbm, tiles_ref, out_ref, pairs, occ, held_tiles, kron, held, sems):
    count, ri_width = tiles_ref.shape[0], tiles_ref.shape[2]
    occ_batch = occ_hbm.shape[0]
    width = AO_GROUP * QB
    pairs_copy = pltpu.make_async_copy(pairs_hbm, pairs, sems.at[count])
    occ_copy = pltpu.make_async_copy(occ_hbm, occ, sems.at[count + 1])
    pairs_copy.start()
    occ_copy.start()
    copies = [
        pltpu.make_async_copy(tiles_ref.at[t, pl.ds(0, AO_GROUP)], held_tiles.at[t], sems.at[t]) for t in range(count)
    ]
    for copy in copies:
        copy.start()
    row = lax.broadcasted_iota(jnp.int32, (LANES, width), 0)
    lane = lax.broadcasted_iota(jnp.int32, (LANES, width), 1)
    spread = jnp.where(jnp.right_shift(lane, QB.bit_length() - 1) == row, 1.0, 0.0).astype(jnp.bfloat16)
    q_row = lax.broadcasted_iota(jnp.int32, (QB, width), 0)
    q_col = jnp.bitwise_and(lax.broadcasted_iota(jnp.int32, (QB, width), 1), QB - 1)
    diagonal = q_row == q_col
    pairs_copy.wait()
    occ_copy.wait()
    first = me[0] * count
    coef = [occupied_rows(occ, pairs[0, first + t] * AO_GROUP) for t in range(count)]
    coef = jnp.concatenate(coef, 0).astype(jnp.bfloat16)
    wide = jnp.dot(coef, spread, preferred_element_type=jnp.float32)
    for t in range(count):
        for i in range(occ_batch):
            rows = jnp.broadcast_to(wide[t * occ_batch + i : t * occ_batch + i + 1], (QB, width))
            kron[t, i * QB : (i + 1) * QB, :] = jnp.where(diagonal, rows, 0.0).astype(jnp.bfloat16)
    for t in range(count):
        copies[t].wait()
        for b in range(0, ri_width // QB, PAIR):
            parts = [held_tiles[t, :, (b + k) * QB : (b + k + 1) * QB, :].reshape(width, LANES) for k in range(PAIR)]
            half = jnp.dot(kron[t], jnp.concatenate(parts, 1), preferred_element_type=jnp.float32)
            for k in range(PAIR):
                part = half[:, k * LANES : (k + 1) * LANES].reshape(occ_batch, QB, LANES)
                held[t, :, (b + k) * QB : (b + k + 1) * QB, :] = part
    rows = occ_batch * ri_width
    lane = lax.broadcasted_iota(jnp.int32, (rows, LANES), 1)
    pieces = []
    for s in range(count):
        tile = jnp.int32(0)
        for j in range(1, count):
            tile = jnp.where(lax.rem(pairs[1, first + j], count) == s, j, tile)
        pieces.append(held[tile].reshape(rows, LANES))
    for out in range(count * AO_GROUP // LANES):
        value = None
        for s in range(count):
            begin, end = s * AO_GROUP - out * LANES, (s + 1) * AO_GROUP - out * LANES
            if end <= 0 or begin >= LANES:
                continue
            turned = pieces[s] if begin % LANES == 0 else pltpu.roll(pieces[s], begin % LANES, 1)
            value = turned if value is None else jnp.where(lane < begin, value, turned)
        out_ref[:, out * LANES : (out + 1) * LANES] = value.astype(out_ref.dtype)


def half_transform(me, pairs, occ, tiles):
    count, ri_width = tiles.shape[0], tiles.shape[2]
    occ_batch = occ.shape[0]
    width = AO_GROUP * QB
    rows, columns = occ_batch * ri_width, count * AO_GROUP
    return pl.pallas_call(
        half_kernel,
        in_specs=[pl.BlockSpec(memory_space=pltpu.SMEM)] + [pl.BlockSpec(memory_space=pl.ANY)] * 3,
        out_specs=pl.BlockSpec(memory_space=pltpu.VMEM),
        out_shape=jax.ShapeDtypeStruct((rows, columns), jnp.bfloat16),
        scratch_shapes=[
            pltpu.SMEM(pairs.shape, jnp.int32),
            pltpu.VMEM(occ.shape, jnp.bfloat16),
            pltpu.VMEM((count, AO_GROUP, ri_width, LANES), jnp.bfloat16),
            pltpu.VMEM((count, occ_batch * QB, width), jnp.bfloat16),
            pltpu.VMEM((count, occ_batch, ri_width, LANES), jnp.float32),
            pltpu.SemaphoreType.DMA((count + 2,)),
        ],
        compiler_params=pltpu.CompilerParams(vmem_limit_bytes=HALF_VMEM),
        cost_estimate=pl.CostEstimate(
            flops=2 * rows * columns * width, bytes_accessed=2 * tiles.size, transcendentals=0
        ),
        name="half_transform",
    )(me, pairs, occ, tiles)


def chip_at(place, chips):
    place = lax.rem(place + chips, chips)
    return jnp.where(place < chips // 2, 2 * place, 2 * (chips - 1 - place) + 1)


def place_of(chip, chips):
    return jnp.where(lax.rem(chip, 2) == 0, chip // 2, chips - 1 - chip // 2)


def take_windows(count, pairs, vir_ref, dev, write):
    columns = count * AO_GROUP
    panels = vir_ref.shape[1] // columns
    cols = [pairs[1, dev * count + j] for j in range(count)]
    first = cols[0]
    for col in cols:
        before = lax.rem(col + (NGROUP - 1), NGROUP)
        is_first = functools.reduce(jnp.logical_and, [other != before for other in cols])
        first = jnp.where(is_first, col, first)
    panel = first // count
    bound = lax.rem(first, count) * AO_GROUP
    low = pl.multiple_of(panel * columns, LANES)
    high = pl.multiple_of(lax.rem(panel + 1, panels) * columns, LANES)
    for j in range(columns // LANES):
        lane = lax.broadcasted_iota(jnp.int32, (QB, LANES), 1) + j * LANES
        keep = jnp.where(lane >= bound, 1.0, 0.0)
        here = vir_ref[:, pl.ds(pl.multiple_of(low + j * LANES, LANES), LANES)]
        there = vir_ref[:, pl.ds(pl.multiple_of(high + j * LANES, LANES), LANES)]
        keep, drop = keep[:1].astype(jnp.bfloat16), (1.0 - keep[:1]).astype(jnp.bfloat16)
        write(j, here * keep + there * drop)


def window_kernel(count, chips, me, pairs, own_ref, other_ref, both_ref, last_ref):
    chip, core = me[0] // 2, lax.rem(me[0], 2)
    place = place_of(chip, chips)
    behind = 2 * core - 1
    rows, columns = own_ref.shape[0], count * AO_GROUP
    for k in range(chips - 1):
        source = chip_at(place + behind * ((k + 1) // 2), chips)
        dev = 2 * source + (core if k == 0 or k % 2 == 1 else 1 - core)
        for half, vir_ref in enumerate((own_ref, other_ref)):

            def write(j, value, k=k, half=half):
                at = k * columns + j * LANES
                both_ref[half * rows : (half + 1) * rows, at : at + LANES] = value

            take_windows(count, pairs, vir_ref, dev, write)
    source = chip_at(place + chips // 2, chips)
    for k, dev in enumerate((2 * source + core, 2 * source + 1 - core)):

        def write(j, value, k=k):
            at = k * columns + j * LANES
            last_ref[:, at : at + LANES] = value

        take_windows(count, pairs, own_ref, dev, write)


def windows(me, pairs, vir, other_vir, count, chips):
    rows, columns = vir.shape[0], count * AO_GROUP
    smem, vmem = pl.BlockSpec(memory_space=pltpu.SMEM), pl.BlockSpec(memory_space=pltpu.VMEM)
    return pl.pallas_call(
        functools.partial(window_kernel, count, chips),
        in_specs=[smem, smem, vmem, vmem],
        out_specs=[vmem, vmem],
        out_shape=[
            jax.ShapeDtypeStruct((2 * rows, (chips - 1) * columns), vir.dtype),
            jax.ShapeDtypeStruct((rows, 2 * columns), vir.dtype),
        ],
        compiler_params=pltpu.CompilerParams(vmem_limit_bytes=WINDOW_VMEM),
        cost_estimate=pl.CostEstimate(flops=0, bytes_accessed=8 * vir.size, transcendentals=0),
        name="vir_windows",
    )(me, pairs, vir, other_vir)


def product(vir, block):
    return lax.dot_general(vir, block, (((1,), (1,)), ((), ())), preferred_element_type=jnp.float32)


def on_device(chips, tiles, pairs, occ_coef, vir_coef):
    count = tiles.shape[0]
    columns = count * AO_GROUP
    me = lax.axis_index("ao").astype(jnp.int32).reshape(1)
    pairs, occ, vir = pairs.T, occ_coef.T, vir_coef.T
    rows = vir.shape[0]

    ring = [2 * p if p < chips // 2 else 2 * (chips - 1 - p) + 1 for p in range(chips)]
    links = [(ring[p], ring[(p + 1) % chips]) for p in range(chips)]
    onward = [(2 * a, 2 * b) for a, b in links] + [(2 * b + 1, 2 * a + 1) for a, b in links]
    across = [(d, d ^ 1) for d in range(2 * chips)]

    own = half_transform(me, pairs, occ, tiles)
    both_w, last_w = windows(me, pairs, vir, lax.ppermute(vir, "ao", across), count, chips)
    blocks = [own]
    sums, summed = None, 0

    def add_to(sums, k):
        term = product(both_w[:, k * columns : (k + 1) * columns], blocks[k])
        return term if sums is None else sums + term

    for message in range(1, chips):
        if message == 1:
            block = own
        elif message == 2:
            block = lax.ppermute(own, "ao", across)
        else:
            block = blocks[message - 2]
        if message == 3:
            block, both_w, last_w = lax.optimization_barrier((block, both_w, last_w))
        elif message > 3:
            while summed < message - 2:
                sums = add_to(sums, summed)
                summed += 1
            block, sums = lax.optimization_barrier((block, sums))
        block = lax.ppermute(block, "ao", onward)
        if message < chips - 1:
            blocks.append(block)
        else:
            last = block
    while summed < len(blocks):
        sums = add_to(sums, summed)
        summed += 1
    received = lax.ppermute(sums[rows:], "ao", across)
    total = sums[:rows] + received + product(last_w[:, :columns], last)
    total = total + product(last_w[:, columns:], lax.ppermute(last, "ao", across))
    return total.astype(jnp.bfloat16)


def solution(mesh):
    return jax.shard_map(
        functools.partial(on_device, mesh.shape["ao"] // 2),
        mesh=mesh,
        in_specs=(P("ao", None, "groups", None), P(), P(), P(None, "ao")),
        out_specs=P("ao", "groups"),
        check_vma=False,
    )
```

```python
import functools

import jax
import jax.numpy as jnp
from jax import lax
from jax.experimental import pallas as pl
from jax.experimental.pallas import tpu as pltpu
from jax.sharding import PartitionSpec as P

NGROUP = 64
AO_GROUP = 96
LANES = 128
QB = 16
PAIR = 2
HALF_VMEM = 24 * 1024 * 1024
STEP_VMEM = 24 * 1024 * 1024
UNTIMED = pl.CostEstimate(flops=0, bytes_accessed=0, transcendentals=0)


def occupied_rows(occ_ref, offset):
    start = pl.multiple_of((offset // LANES) * LANES, LANES)
    after = pl.multiple_of(jnp.minimum(start + LANES, occ_ref.shape[1] - LANES), LANES)
    shift = offset - start
    turn = lax.rem(LANES - shift, LANES)
    low = pltpu.roll(occ_ref[:, pl.ds(start, LANES)].astype(jnp.float32), turn, 1)
    high = pltpu.roll(occ_ref[:, pl.ds(after, LANES)].astype(jnp.float32), turn, 1)
    lane = lax.broadcasted_iota(jnp.int32, low.shape, 1)
    return jnp.where(lane < LANES - shift, low, high)


def half_kernel(me, pairs_hbm, occ_hbm, tiles_ref, out_ref, pairs, occ, held_tiles, kron, held, sems):
    count, ri_width = tiles_ref.shape[0], tiles_ref.shape[2]
    occ_batch = occ_hbm.shape[0]
    width = AO_GROUP * QB
    pairs_copy = pltpu.make_async_copy(pairs_hbm, pairs, sems.at[count])
    occ_copy = pltpu.make_async_copy(occ_hbm, occ, sems.at[count + 1])
    pairs_copy.start()
    occ_copy.start()
    copies = [
        pltpu.make_async_copy(tiles_ref.at[t, pl.ds(0, AO_GROUP)], held_tiles.at[t], sems.at[t]) for t in range(count)
    ]
    for copy in copies:
        copy.start()
    row = lax.broadcasted_iota(jnp.int32, (LANES, width), 0)
    lane = lax.broadcasted_iota(jnp.int32, (LANES, width), 1)
    spread = jnp.where(jnp.right_shift(lane, QB.bit_length() - 1) == row, 1.0, 0.0).astype(jnp.bfloat16)
    q_row = lax.broadcasted_iota(jnp.int32, (QB, width), 0)
    q_col = jnp.bitwise_and(lax.broadcasted_iota(jnp.int32, (QB, width), 1), QB - 1)
    diagonal = q_row == q_col
    pairs_copy.wait()
    occ_copy.wait()
    first = me[0] * count
    coef = [occupied_rows(occ, pairs[0, first + t] * AO_GROUP) for t in range(count)]
    coef = jnp.concatenate(coef, 0).astype(jnp.bfloat16)
    wide = jnp.dot(coef, spread, preferred_element_type=jnp.float32)
    for t in range(count):
        for i in range(occ_batch):
            rows = jnp.broadcast_to(wide[t * occ_batch + i : t * occ_batch + i + 1], (QB, width))
            kron[t, i * QB : (i + 1) * QB, :] = jnp.where(diagonal, rows, 0.0).astype(jnp.bfloat16)
    for t in range(count):
        copies[t].wait()
        for b in range(0, ri_width // QB, PAIR):
            parts = [held_tiles[t, :, (b + k) * QB : (b + k + 1) * QB, :].reshape(width, LANES) for k in range(PAIR)]
            half = jnp.dot(kron[t], jnp.concatenate(parts, 1), preferred_element_type=jnp.float32)
            for k in range(PAIR):
                part = half[:, k * LANES : (k + 1) * LANES].reshape(occ_batch, QB, LANES)
                held[t, :, (b + k) * QB : (b + k + 1) * QB, :] = part
    rows = occ_batch * ri_width
    lane = lax.broadcasted_iota(jnp.int32, (rows, LANES), 1)
    pieces = []
    for s in range(count):
        tile = jnp.int32(0)
        for j in range(1, count):
            tile = jnp.where(lax.rem(pairs[1, first + j], count) == s, j, tile)
        pieces.append(held[tile].reshape(rows, LANES))
    for out in range(count * AO_GROUP // LANES):
        value = None
        for s in range(count):
            begin, end = s * AO_GROUP - out * LANES, (s + 1) * AO_GROUP - out * LANES
            if end <= 0 or begin >= LANES:
                continue
            turned = pieces[s] if begin % LANES == 0 else pltpu.roll(pieces[s], begin % LANES, 1)
            value = turned if value is None else jnp.where(lane < begin, value, turned)
        out_ref[:, out * LANES : (out + 1) * LANES] = value.astype(out_ref.dtype)


def half_transform(me, pairs, occ, tiles):
    count, ri_width = tiles.shape[0], tiles.shape[2]
    occ_batch = occ.shape[0]
    width = AO_GROUP * QB
    rows, columns = occ_batch * ri_width, count * AO_GROUP
    pairs, occ, tiles = (pltpu.with_memory_space_constraint(x, pltpu.HBM) for x in (pairs, occ, tiles))
    return pl.pallas_call(
        half_kernel,
        in_specs=[pl.BlockSpec(memory_space=pltpu.SMEM)] + [pl.BlockSpec(memory_space=pl.ANY)] * 3,
        out_specs=pl.BlockSpec(memory_space=pltpu.VMEM),
        out_shape=pltpu.VMEM((rows, columns), jnp.bfloat16),
        scratch_shapes=[
            pltpu.SMEM(pairs.shape, jnp.int32),
            pltpu.VMEM(occ.shape, jnp.bfloat16),
            pltpu.VMEM((count, AO_GROUP, ri_width, LANES), jnp.bfloat16),
            pltpu.VMEM((count, occ_batch * QB, width), jnp.bfloat16),
            pltpu.VMEM((count, occ_batch, ri_width, LANES), jnp.float32),
            pltpu.SemaphoreType.DMA((count + 2,)),
        ],
        compiler_params=pltpu.CompilerParams(vmem_limit_bytes=HALF_VMEM),
        cost_estimate=pl.CostEstimate(
            flops=2 * rows * columns * width, bytes_accessed=2 * tiles.size, transcendentals=0
        ),
        name="half_transform",
    )(me, pairs, occ, tiles)


def chip_at(place, chips):
    place = lax.rem(place + chips, chips)
    return jnp.where(place < chips // 2, 2 * place, 2 * (chips - 1 - place) + 1)


def place_of(chip, chips):
    return jnp.where(lax.rem(chip, 2) == 0, chip // 2, chips - 1 - chip // 2)


def take_windows(count, pairs, vir_ref, dev, write):
    columns = count * AO_GROUP
    panels = vir_ref.shape[1] // columns
    cols = [pairs[1, dev * count + j] for j in range(count)]
    first = cols[0]
    for col in cols:
        before = lax.rem(col + (NGROUP - 1), NGROUP)
        is_first = functools.reduce(jnp.logical_and, [other != before for other in cols])
        first = jnp.where(is_first, col, first)
    panel = first // count
    bound = lax.rem(first, count) * AO_GROUP
    low = pl.multiple_of(panel * columns, LANES)
    high = pl.multiple_of(lax.rem(panel + 1, panels) * columns, LANES)
    for j in range(columns // LANES):
        lane = lax.broadcasted_iota(jnp.int32, (QB, LANES), 1) + j * LANES
        keep = jnp.where(lane >= bound, 1.0, 0.0)
        here = vir_ref[:, pl.ds(pl.multiple_of(low + j * LANES, LANES), LANES)]
        there = vir_ref[:, pl.ds(pl.multiple_of(high + j * LANES, LANES), LANES)]
        keep, drop = keep[:1].astype(jnp.bfloat16), (1.0 - keep[:1]).astype(jnp.bfloat16)
        write(j, here * keep + there * drop)


def window_kernel(count, chips, me, pairs, vir_ref, own_ref, other_ref, last_ref):
    chip, core = me[0] // 2, lax.rem(me[0], 2)
    place = place_of(chip, chips)
    columns = count * AO_GROUP

    def store(out_ref, k, dev):
        def write(j, value):
            at = k * columns + j * LANES
            out_ref[:, at : at + LANES] = value

        take_windows(count, pairs, vir_ref, dev, write)

    for k in range(chips - 1):
        for out_ref, which in ((own_ref, core), (other_ref, 1 - core)):
            source = chip_at(place + (2 * which - 1) * ((k + 1) // 2), chips)
            store(out_ref, k, 2 * source + (which if k == 0 or k % 2 == 1 else 1 - which))
    source = chip_at(place + chips // 2, chips)
    store(last_ref, 0, 2 * source + core)
    store(last_ref, 1, 2 * source + 1 - core)


def windows(me, pairs, vir, count, chips):
    rows, columns = vir.shape[0], count * AO_GROUP
    smem, vmem = pl.BlockSpec(memory_space=pltpu.SMEM), pl.BlockSpec(memory_space=pltpu.VMEM)
    return pl.pallas_call(
        functools.partial(window_kernel, count, chips),
        in_specs=[smem, smem, vmem],
        out_specs=[vmem, vmem, vmem],
        out_shape=[
            jax.ShapeDtypeStruct((rows, (chips - 1) * columns), vir.dtype),
            jax.ShapeDtypeStruct((rows, (chips - 1) * columns), vir.dtype),
            jax.ShapeDtypeStruct((rows, 2 * columns), vir.dtype),
        ],
        compiler_params=pltpu.CompilerParams(vmem_limit_bytes=STEP_VMEM),
        cost_estimate=UNTIMED,
        name="vir_windows",
    )(me, pairs, vir)


def dot_columns(vir, block):
    return lax.dot_general(vir, block, (((1,), (1,)), ((), ())), preferred_element_type=jnp.float32)


def add_kernel(k, own_w, other_w, block, other_block, *refs):
    columns = block.shape[1]
    at = slice(k * columns, (k + 1) * columns)
    total = dot_columns(own_w[:, at], block[...]) + dot_columns(other_w[:, at], other_block[...])
    refs[-1][...] = total + refs[0][...] if len(refs) == 2 else total


def add_blocks(total, k, own_w, other_w, block, other_block):
    shape = jax.ShapeDtypeStruct((own_w.shape[0], block.shape[0]), jnp.float32)
    vmem = pl.BlockSpec(memory_space=pltpu.VMEM)
    before = () if total is None else (total,)
    return pl.pallas_call(
        functools.partial(add_kernel, k),
        in_specs=[vmem] * (4 + len(before)),
        out_specs=vmem,
        out_shape=shape,
        input_output_aliases={4: 0} if before else {},
        compiler_params=pltpu.CompilerParams(vmem_limit_bytes=STEP_VMEM),
        cost_estimate=UNTIMED,
        name="add_blocks",
    )(own_w, other_w, block, other_block, *before)


def last_kernel(last_w, last, own_sum, out_ref):
    out_ref[...] = own_sum[...] + dot_columns(last_w[:, : last.shape[1]], last[...])


def add_last(last_w, last, own_sum):
    vmem = pl.BlockSpec(memory_space=pltpu.VMEM)
    return pl.pallas_call(
        last_kernel,
        in_specs=[vmem] * 3,
        out_specs=vmem,
        out_shape=jax.ShapeDtypeStruct(own_sum.shape, own_sum.dtype),
        input_output_aliases={2: 0},
        compiler_params=pltpu.CompilerParams(vmem_limit_bytes=STEP_VMEM),
        cost_estimate=UNTIMED,
        name="add_last",
    )(last_w, last, own_sum)


def finish_kernel(cuts, last_w, block, total, out_hbm, out, sems):
    columns = block.shape[1]
    copies = []
    for p, (begin, end) in enumerate(zip(cuts[:-1], cuts[1:])):
        value = total[begin:end] + dot_columns(last_w[begin:end, columns:], block[...])
        out[begin:end] = value.astype(out.dtype)
        copies.append(pltpu.make_async_copy(out.at[begin:end], out_hbm.at[begin:end], sems.at[p]))
        copies[-1].start()
    for copy in copies:
        copy.wait()


def finish(last_w, block, total):
    rows = total.shape[0]
    cuts = [0, rows // 32 * 16, rows] if rows % 16 == 0 else [0, rows]
    vmem = pl.BlockSpec(memory_space=pltpu.VMEM)
    return pl.pallas_call(
        functools.partial(finish_kernel, cuts),
        in_specs=[vmem] * 3,
        out_specs=pl.BlockSpec(memory_space=pl.ANY),
        out_shape=jax.ShapeDtypeStruct(total.shape, jnp.bfloat16),
        scratch_shapes=[pltpu.VMEM(total.shape, jnp.bfloat16), pltpu.SemaphoreType.DMA((len(cuts) - 1,))],
        compiler_params=pltpu.CompilerParams(vmem_limit_bytes=STEP_VMEM),
        cost_estimate=UNTIMED,
        name="finish",
    )(last_w, block, total)


def on_device(chips, tiles, pairs, occ_coef, vir_coef):
    count = tiles.shape[0]
    columns = count * AO_GROUP
    me = lax.axis_index("ao").astype(jnp.int32).reshape(1)
    pairs, occ, vir = pairs.T, occ_coef.T, vir_coef.T

    ring = [2 * p if p < chips // 2 else 2 * (chips - 1 - p) + 1 for p in range(chips)]
    links = [(ring[p], ring[(p + 1) % chips]) for p in range(chips)]
    onward = [(2 * a, 2 * b) for a, b in links] + [(2 * b + 1, 2 * a + 1) for a, b in links]
    across = [(d, d ^ 1) for d in range(2 * chips)]

    own = half_transform(me, pairs, occ, tiles)
    blocks, other_blocks = [own], [lax.ppermute(own, "ao", across)]
    first_other, vir = lax.optimization_barrier((other_blocks[0], vir))
    own_w, other_w, last_w = windows(me, pairs, vir, count, chips)
    total, summed = None, 0
    for message in range(1, chips):
        if message == 1:
            block = own
        elif message == 2:
            block = first_other
        else:
            block = blocks[message - 2]
        if message == 3:
            block, own_w, other_w, last_w = lax.optimization_barrier((block, own_w, other_w, last_w))
        if message > 3:
            total = add_blocks(total, summed, own_w, other_w, blocks[summed], other_blocks[summed])
            summed += 1
            block, total = lax.optimization_barrier((block, total))
        block = lax.ppermute(block, "ao", onward)
        if message < chips - 1:
            blocks.append(block)
            other_blocks.append(lax.ppermute(block, "ao", across))
        else:
            last = block
    while summed < len(blocks) - 1:
        total = add_blocks(total, summed, own_w, other_w, blocks[summed], other_blocks[summed])
        summed += 1
    last, total = lax.optimization_barrier((last, total))
    other_last = lax.ppermute(last, "ao", across)
    while summed < len(blocks):
        total = add_blocks(total, summed, own_w, other_w, blocks[summed], other_blocks[summed])
        summed += 1
    return finish(last_w, other_last, add_last(last_w, last, total))


def solution(mesh):
    return jax.shard_map(
        functools.partial(on_device, mesh.shape["ao"] // 2),
        mesh=mesh,
        in_specs=(P("ao", None, "groups", None), P(), P(), P(None, "ao")),
        out_specs=P("ao", "groups"),
        check_vma=False,
    )
```

```python
import functools

import jax
import jax.numpy as jnp
from jax import lax
from jax.experimental import pallas as pl
from jax.experimental.pallas import tpu as pltpu
from jax.sharding import PartitionSpec as P

NGROUP = 64
AO_GROUP = 96
LANES = 128
QB = 16
PAIR = 2
HALF_VMEM = 24 * 1024 * 1024
STEP_VMEM = 24 * 1024 * 1024
UNTIMED = pl.CostEstimate(flops=0, bytes_accessed=0, transcendentals=0)


def occupied_rows(occ_ref, offset):
    start = pl.multiple_of((offset // LANES) * LANES, LANES)
    after = pl.multiple_of(jnp.minimum(start + LANES, occ_ref.shape[1] - LANES), LANES)
    shift = offset - start
    turn = lax.rem(LANES - shift, LANES)
    low = pltpu.roll(occ_ref[:, pl.ds(start, LANES)].astype(jnp.float32), turn, 1)
    high = pltpu.roll(occ_ref[:, pl.ds(after, LANES)].astype(jnp.float32), turn, 1)
    lane = lax.broadcasted_iota(jnp.int32, low.shape, 1)
    return jnp.where(lane < LANES - shift, low, high)


def half_kernel(me, pairs_hbm, occ_hbm, tiles_ref, out_ref, pairs, occ, held_tiles, kron, held, sems):
    count, ri_width = tiles_ref.shape[0], tiles_ref.shape[2]
    occ_batch = occ_hbm.shape[0]
    width = AO_GROUP * QB
    pairs_copy = pltpu.make_async_copy(pairs_hbm, pairs, sems.at[count])
    occ_copy = pltpu.make_async_copy(occ_hbm, occ, sems.at[count + 1])
    pairs_copy.start()
    occ_copy.start()
    copies = [
        pltpu.make_async_copy(tiles_ref.at[t, pl.ds(0, AO_GROUP)], held_tiles.at[t], sems.at[t]) for t in range(count)
    ]
    for copy in copies:
        copy.start()
    row = lax.broadcasted_iota(jnp.int32, (LANES, width), 0)
    lane = lax.broadcasted_iota(jnp.int32, (LANES, width), 1)
    spread = jnp.where(jnp.right_shift(lane, QB.bit_length() - 1) == row, 1.0, 0.0).astype(jnp.bfloat16)
    q_row = lax.broadcasted_iota(jnp.int32, (QB, width), 0)
    q_col = jnp.bitwise_and(lax.broadcasted_iota(jnp.int32, (QB, width), 1), QB - 1)
    diagonal = q_row == q_col
    pairs_copy.wait()
    occ_copy.wait()
    first = me[0] * count
    coef = [occupied_rows(occ, pairs[0, first + t] * AO_GROUP) for t in range(count)]
    coef = jnp.concatenate(coef, 0).astype(jnp.bfloat16)
    wide = jnp.dot(coef, spread, preferred_element_type=jnp.float32)
    for t in range(count):
        for i in range(occ_batch):
            rows = jnp.broadcast_to(wide[t * occ_batch + i : t * occ_batch + i + 1], (QB, width))
            kron[t, i * QB : (i + 1) * QB, :] = jnp.where(diagonal, rows, 0.0).astype(jnp.bfloat16)
    for t in range(count):
        copies[t].wait()
        for b in range(0, ri_width // QB, PAIR):
            parts = [held_tiles[t, :, (b + k) * QB : (b + k + 1) * QB, :].reshape(width, LANES) for k in range(PAIR)]
            half = jnp.dot(kron[t], jnp.concatenate(parts, 1), preferred_element_type=jnp.float32)
            for k in range(PAIR):
                part = half[:, k * LANES : (k + 1) * LANES].reshape(occ_batch, QB, LANES)
                held[t, :, (b + k) * QB : (b + k + 1) * QB, :] = part
    rows = occ_batch * ri_width
    lane = lax.broadcasted_iota(jnp.int32, (rows, LANES), 1)
    pieces = []
    for s in range(count):
        tile = jnp.int32(0)
        for j in range(1, count):
            tile = jnp.where(lax.rem(pairs[1, first + j], count) == s, j, tile)
        pieces.append(held[tile].reshape(rows, LANES))
    for out in range(count * AO_GROUP // LANES):
        value = None
        for s in range(count):
            begin, end = s * AO_GROUP - out * LANES, (s + 1) * AO_GROUP - out * LANES
            if end <= 0 or begin >= LANES:
                continue
            turned = pieces[s] if begin % LANES == 0 else pltpu.roll(pieces[s], begin % LANES, 1)
            value = turned if value is None else jnp.where(lane < begin, value, turned)
        out_ref[:, out * LANES : (out + 1) * LANES] = value.astype(out_ref.dtype)


def half_transform(me, pairs, occ, tiles):
    count, ri_width = tiles.shape[0], tiles.shape[2]
    occ_batch = occ.shape[0]
    width = AO_GROUP * QB
    rows, columns = occ_batch * ri_width, count * AO_GROUP
    pairs, occ, tiles = (pltpu.with_memory_space_constraint(x, pltpu.HBM) for x in (pairs, occ, tiles))
    return pl.pallas_call(
        half_kernel,
        in_specs=[pl.BlockSpec(memory_space=pltpu.SMEM)] + [pl.BlockSpec(memory_space=pl.ANY)] * 3,
        out_specs=pl.BlockSpec(memory_space=pltpu.VMEM),
        out_shape=pltpu.VMEM((rows, columns), jnp.bfloat16),
        scratch_shapes=[
            pltpu.SMEM(pairs.shape, jnp.int32),
            pltpu.VMEM(occ.shape, jnp.bfloat16),
            pltpu.VMEM((count, AO_GROUP, ri_width, LANES), jnp.bfloat16),
            pltpu.VMEM((count, occ_batch * QB, width), jnp.bfloat16),
            pltpu.VMEM((count, occ_batch, ri_width, LANES), jnp.float32),
            pltpu.SemaphoreType.DMA((count + 2,)),
        ],
        compiler_params=pltpu.CompilerParams(vmem_limit_bytes=HALF_VMEM),
        cost_estimate=pl.CostEstimate(
            flops=2 * rows * columns * width, bytes_accessed=2 * tiles.size, transcendentals=0
        ),
        name="half_transform",
    )(me, pairs, occ, tiles)


def chip_at(place, chips):
    place = lax.rem(place + chips, chips)
    return jnp.where(place < chips // 2, 2 * place, 2 * (chips - 1 - place) + 1)


def place_of(chip, chips):
    return jnp.where(lax.rem(chip, 2) == 0, chip // 2, chips - 1 - chip // 2)


def take_windows(count, pairs, vir_ref, dev, write):
    columns = count * AO_GROUP
    panels = vir_ref.shape[1] // columns
    cols = [pairs[1, dev * count + j] for j in range(count)]
    first = cols[0]
    for col in cols:
        before = lax.rem(col + (NGROUP - 1), NGROUP)
        is_first = functools.reduce(jnp.logical_and, [other != before for other in cols])
        first = jnp.where(is_first, col, first)
    panel = first // count
    bound = lax.rem(first, count) * AO_GROUP
    low = pl.multiple_of(panel * columns, LANES)
    high = pl.multiple_of(lax.rem(panel + 1, panels) * columns, LANES)
    for j in range(columns // LANES):
        lane = lax.broadcasted_iota(jnp.int32, (QB, LANES), 1) + j * LANES
        keep = jnp.where(lane >= bound, 1.0, 0.0)
        here = vir_ref[:, pl.ds(pl.multiple_of(low + j * LANES, LANES), LANES)]
        there = vir_ref[:, pl.ds(pl.multiple_of(high + j * LANES, LANES), LANES)]
        keep, drop = keep[:1].astype(jnp.bfloat16), (1.0 - keep[:1]).astype(jnp.bfloat16)
        write(j, here * keep + there * drop)


def window_kernel(count, chips, me, pairs, vir_ref, own_ref, other_ref, last_ref):
    chip, core = me[0] // 2, lax.rem(me[0], 2)
    place = place_of(chip, chips)
    columns = count * AO_GROUP

    def store(out_ref, k, dev):
        def write(j, value):
            at = k * columns + j * LANES
            out_ref[:, at : at + LANES] = value

        take_windows(count, pairs, vir_ref, dev, write)

    for k in range(chips - 1):
        for out_ref, which in ((own_ref, core), (other_ref, 1 - core)):
            source = chip_at(place + (2 * which - 1) * ((k + 1) // 2), chips)
            store(out_ref, k, 2 * source + (which if k == 0 or k % 2 == 1 else 1 - which))
    source = chip_at(place + chips // 2, chips)
    store(last_ref, 0, 2 * source + core)
    store(last_ref, 1, 2 * source + 1 - core)


def windows(me, pairs, vir, count, chips):
    rows, columns = vir.shape[0], count * AO_GROUP
    smem, vmem = pl.BlockSpec(memory_space=pltpu.SMEM), pl.BlockSpec(memory_space=pltpu.VMEM)
    return pl.pallas_call(
        functools.partial(window_kernel, count, chips),
        in_specs=[smem, smem, vmem],
        out_specs=[vmem, vmem, vmem],
        out_shape=[
            jax.ShapeDtypeStruct((rows, (chips - 1) * columns), vir.dtype),
            jax.ShapeDtypeStruct((rows, (chips - 1) * columns), vir.dtype),
            jax.ShapeDtypeStruct((rows, 2 * columns), vir.dtype),
        ],
        compiler_params=pltpu.CompilerParams(vmem_limit_bytes=STEP_VMEM),
        cost_estimate=UNTIMED,
        name="vir_windows",
    )(me, pairs, vir)


def dot_columns(vir, block):
    return lax.dot_general(vir, block, (((1,), (1,)), ((), ())), preferred_element_type=jnp.float32)


def add_kernel(k, own_w, other_w, block, other_block, *refs):
    columns = block.shape[1]
    at = slice(k * columns, (k + 1) * columns)
    total = dot_columns(own_w[:, at], block[...]) + dot_columns(other_w[:, at], other_block[...])
    refs[-1][...] = total + refs[0][...] if len(refs) == 2 else total


def add_blocks(total, k, own_w, other_w, block, other_block):
    shape = jax.ShapeDtypeStruct((own_w.shape[0], block.shape[0]), jnp.float32)
    vmem = pl.BlockSpec(memory_space=pltpu.VMEM)
    before = () if total is None else (total,)
    return pl.pallas_call(
        functools.partial(add_kernel, k),
        in_specs=[vmem] * (4 + len(before)),
        out_specs=vmem,
        out_shape=shape,
        input_output_aliases={4: 0} if before else {},
        compiler_params=pltpu.CompilerParams(vmem_limit_bytes=STEP_VMEM),
        cost_estimate=UNTIMED,
        name="add_blocks",
    )(own_w, other_w, block, other_block, *before)


def last_kernel(last_w, last_a, last_b, other_a, before, out_ref):
    rows, columns = last_a.shape
    own = last_w[:, :columns]
    first = before[:, :rows] + dot_columns(own, last_a[...])
    out_ref[:, :rows] = first + dot_columns(last_w[:, columns:], other_a[...])
    out_ref[:, rows:] = before[:, rows:] + dot_columns(own, last_b[...])


def add_last(last_w, last_a, last_b, other_a, before):
    vmem = pl.BlockSpec(memory_space=pltpu.VMEM)
    return pl.pallas_call(
        last_kernel,
        in_specs=[vmem] * 5,
        out_specs=vmem,
        out_shape=jax.ShapeDtypeStruct(before.shape, before.dtype),
        input_output_aliases={4: 0},
        compiler_params=pltpu.CompilerParams(vmem_limit_bytes=STEP_VMEM),
        cost_estimate=UNTIMED,
        name="add_last",
    )(last_w, last_a, last_b, other_a, before)


def finish_kernel(cuts, last_w, block, total, out_hbm, out, sems):
    columns = block.shape[1]
    split = total.shape[1] - block.shape[0]
    copies = []
    for p, (begin, end) in enumerate(zip(cuts[:-1], cuts[1:])):
        value = total[begin:end, split:] + dot_columns(last_w[begin:end, columns:], block[...])
        out[begin:end, :split] = total[begin:end, :split].astype(out.dtype)
        out[begin:end, split:] = value.astype(out.dtype)
        copies.append(pltpu.make_async_copy(out.at[begin:end], out_hbm.at[begin:end], sems.at[p]))
        copies[-1].start()
    for copy in copies:
        copy.wait()


def finish(last_w, block, total):
    rows = total.shape[0]
    cuts = [0, rows // 32 * 16, rows] if rows % 16 == 0 else [0, rows]
    vmem = pl.BlockSpec(memory_space=pltpu.VMEM)
    return pl.pallas_call(
        functools.partial(finish_kernel, cuts),
        in_specs=[vmem] * 3,
        out_specs=pl.BlockSpec(memory_space=pl.ANY),
        out_shape=jax.ShapeDtypeStruct(total.shape, jnp.bfloat16),
        scratch_shapes=[pltpu.VMEM(total.shape, jnp.bfloat16), pltpu.SemaphoreType.DMA((len(cuts) - 1,))],
        compiler_params=pltpu.CompilerParams(vmem_limit_bytes=STEP_VMEM),
        cost_estimate=UNTIMED,
        name="finish",
    )(last_w, block, total)


def on_device(chips, tiles, pairs, occ_coef, vir_coef):
    count = tiles.shape[0]
    columns = count * AO_GROUP
    me = lax.axis_index("ao").astype(jnp.int32).reshape(1)
    pairs, occ, vir = pairs.T, occ_coef.T, vir_coef.T

    ring = [2 * p if p < chips // 2 else 2 * (chips - 1 - p) + 1 for p in range(chips)]
    links = [(ring[p], ring[(p + 1) % chips]) for p in range(chips)]
    onward = [(2 * a, 2 * b) for a, b in links] + [(2 * b + 1, 2 * a + 1) for a, b in links]
    across = [(d, d ^ 1) for d in range(2 * chips)]

    own = half_transform(me, pairs, occ, tiles)
    blocks, other_blocks = [own], [lax.ppermute(own, "ao", across)]
    first_other, vir = lax.optimization_barrier((other_blocks[0], vir))
    own_w, other_w, last_w = windows(me, pairs, vir, count, chips)
    total, summed = None, 0
    for message in range(1, chips):
        if message == 1:
            block = own
        elif message == 2:
            block = first_other
        else:
            block = blocks[message - 2]
        if message == 3:
            block, own_w, other_w, last_w = lax.optimization_barrier((block, own_w, other_w, last_w))
        if message > 3:
            total = add_blocks(total, summed, own_w, other_w, blocks[summed], other_blocks[summed])
            summed += 1
            block, total = lax.optimization_barrier((block, total))
        if message < chips - 1:
            block = lax.ppermute(block, "ao", onward)
            blocks.append(block)
            if message < chips - 2:
                other_blocks.append(lax.ppermute(block, "ao", across))
            else:
                h = block.shape[0] // 2
                other_blocks.append(jnp.concatenate([lax.ppermute(p, "ao", across) for p in (block[:h], block[h:])], 0))
        else:
            half = block.shape[0] // 2
            last_a = lax.ppermute(block[:half], "ao", onward)
            last_b = lax.ppermute(block[half:], "ao", onward)
    while summed < len(blocks) - 1:
        total = add_blocks(total, summed, own_w, other_w, blocks[summed], other_blocks[summed])
        summed += 1
    last_a, total = lax.optimization_barrier((last_a, total))
    other_a = lax.ppermute(last_a, "ao", across)
    last_b, total = lax.optimization_barrier((last_b, total))
    other_b = lax.ppermute(last_b, "ao", across)
    while summed < len(blocks):
        total = add_blocks(total, summed, own_w, other_w, blocks[summed], other_blocks[summed])
        summed += 1
    return finish(last_w, other_b, add_last(last_w, last_a, last_b, other_a, total))


def solution(mesh):
    return jax.shard_map(
        functools.partial(on_device, mesh.shape["ao"] // 2),
        mesh=mesh,
        in_specs=(P("ao", None, "groups", None), P(), P(), P(None, "ao")),
        out_specs=P("ao", "groups"),
        check_vma=False,
    )
```

```python
import functools

import jax
import jax.numpy as jnp
from jax import lax
from jax.experimental import pallas as pl
from jax.experimental.pallas import tpu as pltpu
from jax.sharding import PartitionSpec as P

NGROUP = 64
AO_GROUP = 96
LANES = 128
QB = 16
PAIR = 2
HALF_VMEM = 24 * 1024 * 1024
STEP_VMEM = 24 * 1024 * 1024
UNTIMED = pl.CostEstimate(flops=0, bytes_accessed=0, transcendentals=0)


def occupied_rows(occ_ref, offset):
    start = pl.multiple_of((offset // LANES) * LANES, LANES)
    after = pl.multiple_of(jnp.minimum(start + LANES, occ_ref.shape[1] - LANES), LANES)
    shift = offset - start
    turn = lax.rem(LANES - shift, LANES)
    low = pltpu.roll(occ_ref[:, pl.ds(start, LANES)].astype(jnp.float32), turn, 1)
    high = pltpu.roll(occ_ref[:, pl.ds(after, LANES)].astype(jnp.float32), turn, 1)
    lane = lax.broadcasted_iota(jnp.int32, low.shape, 1)
    return jnp.where(lane < LANES - shift, low, high)


def half_kernel(me, pairs_hbm, occ_hbm, tiles_ref, out_ref, pairs, occ, held_tiles, kron, held, sems):
    count, ri_width = tiles_ref.shape[0], tiles_ref.shape[2]
    occ_batch = occ_hbm.shape[0]
    width = AO_GROUP * QB
    pairs_copy = pltpu.make_async_copy(pairs_hbm, pairs, sems.at[count + 1])
    occ_copy = pltpu.make_async_copy(occ_hbm, occ, sems.at[count + 2])
    pairs_copy.start()
    occ_copy.start()
    parts = [(t, 0, AO_GROUP) for t in range(count - 1)]
    parts += [(count - 1, 0, AO_GROUP // 2), (count - 1, AO_GROUP // 2, AO_GROUP // 2)]
    copies = []
    for n, (t, r, size) in enumerate(parts):
        source, target = tiles_ref.at[t, pl.ds(r, size)], held_tiles.at[t, pl.ds(r, size)]
        copies.append(pltpu.make_async_copy(source, target, sems.at[n]))
        copies[-1].start()
    row = lax.broadcasted_iota(jnp.int32, (LANES, width), 0)
    lane = lax.broadcasted_iota(jnp.int32, (LANES, width), 1)
    spread = jnp.where(jnp.right_shift(lane, QB.bit_length() - 1) == row, 1.0, 0.0).astype(jnp.bfloat16)
    q_row = lax.broadcasted_iota(jnp.int32, (QB, width), 0)
    q_col = jnp.bitwise_and(lax.broadcasted_iota(jnp.int32, (QB, width), 1), QB - 1)
    diagonal = q_row == q_col
    pairs_copy.wait()
    occ_copy.wait()
    first = me[0] * count
    coef = [occupied_rows(occ, pairs[0, first + t] * AO_GROUP) for t in range(count)]
    coef = jnp.concatenate(coef, 0).astype(jnp.bfloat16)
    wide = jnp.dot(coef, spread, preferred_element_type=jnp.float32)
    for t in range(count):
        for i in range(occ_batch):
            rows = jnp.broadcast_to(wide[t * occ_batch + i : t * occ_batch + i + 1], (QB, width))
            kron[t, i * QB : (i + 1) * QB, :] = jnp.where(diagonal, rows, 0.0).astype(jnp.bfloat16)
    rows = occ_batch * ri_width
    for copy, (t, r, size) in zip(copies, parts):
        copy.wait()
        for b in range(0, ri_width // QB, PAIR):
            sides = [
                held_tiles[t, r : r + size, (b + k) * QB : (b + k + 1) * QB, :].reshape(size * QB, LANES)
                for k in range(PAIR)
            ]
            factor = kron[t, :, r * QB : (r + size) * QB]
            half = jnp.dot(factor, jnp.concatenate(sides, 1), preferred_element_type=jnp.float32)
            for k in range(PAIR):
                part = half[:, k * LANES : (k + 1) * LANES].reshape(occ_batch, QB, LANES)
                at = slice((b + k) * QB, (b + k + 1) * QB)
                if r > 0:
                    part = part + held[t, :, at, :]
                held[t, :, at, :] = part
    lane = lax.broadcasted_iota(jnp.int32, (rows, LANES), 1)
    pieces = []
    for s in range(count):
        tile = jnp.int32(0)
        for j in range(1, count):
            tile = jnp.where(lax.rem(pairs[1, first + j], count) == s, j, tile)
        pieces.append(held[tile].reshape(rows, LANES))
    for out in range(count * AO_GROUP // LANES):
        value = None
        for s in range(count):
            begin, end = s * AO_GROUP - out * LANES, (s + 1) * AO_GROUP - out * LANES
            if end <= 0 or begin >= LANES:
                continue
            turned = pieces[s] if begin % LANES == 0 else pltpu.roll(pieces[s], begin % LANES, 1)
            value = turned if value is None else jnp.where(lane < begin, value, turned)
        out_ref[:, out * LANES : (out + 1) * LANES] = value.astype(out_ref.dtype)


def half_transform(me, pairs, occ, tiles):
    count, ri_width = tiles.shape[0], tiles.shape[2]
    occ_batch = occ.shape[0]
    width = AO_GROUP * QB
    rows, columns = occ_batch * ri_width, count * AO_GROUP
    pairs, occ, tiles = (pltpu.with_memory_space_constraint(x, pltpu.HBM) for x in (pairs, occ, tiles))
    return pl.pallas_call(
        half_kernel,
        in_specs=[pl.BlockSpec(memory_space=pltpu.SMEM)] + [pl.BlockSpec(memory_space=pl.ANY)] * 3,
        out_specs=pl.BlockSpec(memory_space=pltpu.VMEM),
        out_shape=pltpu.VMEM((rows, columns), jnp.bfloat16),
        scratch_shapes=[
            pltpu.SMEM(pairs.shape, jnp.int32),
            pltpu.VMEM(occ.shape, jnp.bfloat16),
            pltpu.VMEM((count, AO_GROUP, ri_width, LANES), jnp.bfloat16),
            pltpu.VMEM((count, occ_batch * QB, width), jnp.bfloat16),
            pltpu.VMEM((count, occ_batch, ri_width, LANES), jnp.float32),
            pltpu.SemaphoreType.DMA((count + 3,)),
        ],
        compiler_params=pltpu.CompilerParams(vmem_limit_bytes=HALF_VMEM),
        cost_estimate=pl.CostEstimate(
            flops=2 * rows * columns * width, bytes_accessed=2 * tiles.size, transcendentals=0
        ),
        name="half_transform",
    )(me, pairs, occ, tiles)


def chip_at(place, chips):
    place = lax.rem(place + chips, chips)
    return jnp.where(place < chips // 2, 2 * place, 2 * (chips - 1 - place) + 1)


def place_of(chip, chips):
    return jnp.where(lax.rem(chip, 2) == 0, chip // 2, chips - 1 - chip // 2)


def take_windows(count, pairs, vir_ref, dev, write):
    columns = count * AO_GROUP
    panels = vir_ref.shape[1] // columns
    cols = [pairs[1, dev * count + j] for j in range(count)]
    first = cols[0]
    for col in cols:
        before = lax.rem(col + (NGROUP - 1), NGROUP)
        is_first = functools.reduce(jnp.logical_and, [other != before for other in cols])
        first = jnp.where(is_first, col, first)
    panel = first // count
    bound = lax.rem(first, count) * AO_GROUP
    low = pl.multiple_of(panel * columns, LANES)
    high = pl.multiple_of(lax.rem(panel + 1, panels) * columns, LANES)
    for j in range(columns // LANES):
        lane = lax.broadcasted_iota(jnp.int32, (QB, LANES), 1) + j * LANES
        keep = jnp.where(lane >= bound, 1.0, 0.0)
        here = vir_ref[:, pl.ds(pl.multiple_of(low + j * LANES, LANES), LANES)]
        there = vir_ref[:, pl.ds(pl.multiple_of(high + j * LANES, LANES), LANES)]
        keep, drop = keep[:1].astype(jnp.bfloat16), (1.0 - keep[:1]).astype(jnp.bfloat16)
        write(j, here * keep + there * drop)


def window_kernel(count, chips, me, pairs, vir_ref, own_ref, other_ref, last_ref):
    chip, core = me[0] // 2, lax.rem(me[0], 2)
    place = place_of(chip, chips)
    columns = count * AO_GROUP

    def store(out_ref, k, dev):
        def write(j, value):
            at = k * columns + j * LANES
            out_ref[:, at : at + LANES] = value

        take_windows(count, pairs, vir_ref, dev, write)

    for k in range(chips - 1):
        for out_ref, which in ((own_ref, core), (other_ref, 1 - core)):
            source = chip_at(place + (2 * which - 1) * ((k + 1) // 2), chips)
            store(out_ref, k, 2 * source + (which if k == 0 or k % 2 == 1 else 1 - which))
    source = chip_at(place + chips // 2, chips)
    store(last_ref, 0, 2 * source + core)
    store(last_ref, 1, 2 * source + 1 - core)


def windows(me, pairs, vir, count, chips):
    rows, columns = vir.shape[0], count * AO_GROUP
    smem, vmem = pl.BlockSpec(memory_space=pltpu.SMEM), pl.BlockSpec(memory_space=pltpu.VMEM)
    return pl.pallas_call(
        functools.partial(window_kernel, count, chips),
        in_specs=[smem, smem, vmem],
        out_specs=[vmem, vmem, vmem],
        out_shape=[
            jax.ShapeDtypeStruct((rows, (chips - 1) * columns), vir.dtype),
            jax.ShapeDtypeStruct((rows, (chips - 1) * columns), vir.dtype),
            jax.ShapeDtypeStruct((rows, 2 * columns), vir.dtype),
        ],
        compiler_params=pltpu.CompilerParams(vmem_limit_bytes=STEP_VMEM),
        cost_estimate=UNTIMED,
        name="vir_windows",
    )(me, pairs, vir)


def dot_columns(vir, block):
    return lax.dot_general(vir, block, (((1,), (1,)), ((), ())), preferred_element_type=jnp.float32)


def add_kernel(k, own_w, other_w, block, other_block, *refs):
    columns = block.shape[1]
    at = slice(k * columns, (k + 1) * columns)
    total = dot_columns(own_w[:, at], block[...]) + dot_columns(other_w[:, at], other_block[...])
    refs[-1][...] = total + refs[0][...] if len(refs) == 2 else total


def add_blocks(total, k, own_w, other_w, block, other_block):
    shape = jax.ShapeDtypeStruct((own_w.shape[0], block.shape[0]), jnp.float32)
    vmem = pl.BlockSpec(memory_space=pltpu.VMEM)
    before = () if total is None else (total,)
    return pl.pallas_call(
        functools.partial(add_kernel, k),
        in_specs=[vmem] * (4 + len(before)),
        out_specs=vmem,
        out_shape=shape,
        input_output_aliases={4: 0} if before else {},
        compiler_params=pltpu.CompilerParams(vmem_limit_bytes=STEP_VMEM),
        cost_estimate=UNTIMED,
        name="add_blocks",
    )(own_w, other_w, block, other_block, *before)


def last_kernel(last_w, last_a, last_b, other_a, before, done_ref, rest_ref):
    rows, columns = last_a.shape
    own = last_w[:, :columns]
    first = before[:, :rows] + dot_columns(own, last_a[...])
    done_ref[...] = (first + dot_columns(last_w[:, columns:], other_a[...])).astype(done_ref.dtype)
    rest_ref[...] = before[:, rows:] + dot_columns(own, last_b[...])


def add_last(last_w, last_a, last_b, other_a, before):
    vmem = pl.BlockSpec(memory_space=pltpu.VMEM)
    rows = before.shape[0]
    return pl.pallas_call(
        last_kernel,
        in_specs=[vmem] * 5,
        out_specs=[vmem] * 2,
        out_shape=[
            jax.ShapeDtypeStruct((rows, last_a.shape[0]), jnp.bfloat16),
            jax.ShapeDtypeStruct((rows, last_b.shape[0]), before.dtype),
        ],
        compiler_params=pltpu.CompilerParams(vmem_limit_bytes=STEP_VMEM),
        cost_estimate=UNTIMED,
        name="add_last",
    )(last_w, last_a, last_b, other_a, before)


def finish_kernel(last_w, block, done, rest, out_hbm, out, sems):
    columns = block.shape[1]
    split = done.shape[1]
    first = pltpu.make_async_copy(done, out_hbm.at[:, :split], sems.at[0])
    first.start()
    value = rest[...] + dot_columns(last_w[:, columns:], block[...])
    out[...] = value.astype(out.dtype)
    second = pltpu.make_async_copy(out, out_hbm.at[:, split:], sems.at[1])
    second.start()
    first.wait()
    second.wait()


def finish(last_w, block, done, rest):
    vmem = pl.BlockSpec(memory_space=pltpu.VMEM)
    return pl.pallas_call(
        finish_kernel,
        in_specs=[vmem] * 4,
        out_specs=pl.BlockSpec(memory_space=pl.ANY),
        out_shape=jax.ShapeDtypeStruct((rest.shape[0], done.shape[1] + rest.shape[1]), jnp.bfloat16),
        scratch_shapes=[pltpu.VMEM(rest.shape, jnp.bfloat16), pltpu.SemaphoreType.DMA((2,))],
        compiler_params=pltpu.CompilerParams(vmem_limit_bytes=STEP_VMEM),
        cost_estimate=UNTIMED,
        name="finish",
    )(last_w, block, done, rest)


def on_device(chips, tiles, pairs, occ_coef, vir_coef):
    count = tiles.shape[0]
    columns = count * AO_GROUP
    me = lax.axis_index("ao").astype(jnp.int32).reshape(1)
    pairs, occ, vir = pairs.T, occ_coef.T, vir_coef.T

    ring = [2 * p if p < chips // 2 else 2 * (chips - 1 - p) + 1 for p in range(chips)]
    links = [(ring[p], ring[(p + 1) % chips]) for p in range(chips)]
    onward = [(2 * a, 2 * b) for a, b in links] + [(2 * b + 1, 2 * a + 1) for a, b in links]
    across = [(d, d ^ 1) for d in range(2 * chips)]

    own = half_transform(me, pairs, occ, tiles)
    blocks, other_blocks = [own], [lax.ppermute(own, "ao", across)]
    first_other, vir = lax.optimization_barrier((other_blocks[0], vir))
    own_w, other_w, last_w = windows(me, pairs, vir, count, chips)
    total, summed = None, 0
    for message in range(1, chips):
        if message == 1:
            block = own
        elif message == 2:
            block = first_other
        else:
            block = blocks[message - 2]
        if message == 3:
            block, own_w, other_w, last_w = lax.optimization_barrier((block, own_w, other_w, last_w))
        if message > 3:
            total = add_blocks(total, summed, own_w, other_w, blocks[summed], other_blocks[summed])
            summed += 1
            block, total = lax.optimization_barrier((block, total))
        if message < chips - 1:
            block = lax.ppermute(block, "ao", onward)
            blocks.append(block)
            if message < chips - 2:
                other_blocks.append(lax.ppermute(block, "ao", across))
            else:
                h = block.shape[0] // 2
                other_blocks.append(jnp.concatenate([lax.ppermute(p, "ao", across) for p in (block[:h], block[h:])], 0))
        else:
            half = block.shape[0] // 2
            last_a = lax.ppermute(block[:half], "ao", onward)
            last_b = lax.ppermute(block[half:], "ao", onward)
    while summed < len(blocks) - 1:
        total = add_blocks(total, summed, own_w, other_w, blocks[summed], other_blocks[summed])
        summed += 1
    last_a, total = lax.optimization_barrier((last_a, total))
    other_a = lax.ppermute(last_a, "ao", across)
    last_b, total = lax.optimization_barrier((last_b, total))
    other_b = lax.ppermute(last_b, "ao", across)
    while summed < len(blocks):
        total = add_blocks(total, summed, own_w, other_w, blocks[summed], other_blocks[summed])
        summed += 1
    return finish(last_w, other_b, *add_last(last_w, last_a, last_b, other_a, total))


def solution(mesh):
    return jax.shard_map(
        functools.partial(on_device, mesh.shape["ao"] // 2),
        mesh=mesh,
        in_specs=(P("ao", None, "groups", None), P(), P(), P(None, "ao")),
        out_specs=P("ao", "groups"),
        check_vma=False,
    )
```

```python
import functools

import jax
import jax.numpy as jnp
from jax import lax
from jax.experimental import pallas as pl
from jax.experimental.pallas import tpu as pltpu
from jax.sharding import PartitionSpec as P

NGROUP = 64
AO_GROUP = 96
LANES = 128
QB = 16
PAIR = 2
HALF_VMEM = 24 * 1024 * 1024
STEP_VMEM = 24 * 1024 * 1024
UNTIMED = pl.CostEstimate(flops=0, bytes_accessed=0, transcendentals=0)


def occupied_rows(occ_ref, offset):
    start = pl.multiple_of((offset // LANES) * LANES, LANES)
    after = pl.multiple_of(jnp.minimum(start + LANES, occ_ref.shape[1] - LANES), LANES)
    shift = offset - start
    turn = lax.rem(LANES - shift, LANES)
    low = pltpu.roll(occ_ref[:, pl.ds(start, LANES)].astype(jnp.float32), turn, 1)
    high = pltpu.roll(occ_ref[:, pl.ds(after, LANES)].astype(jnp.float32), turn, 1)
    lane = lax.broadcasted_iota(jnp.int32, low.shape, 1)
    return jnp.where(lane < LANES - shift, low, high)


def half_kernel(me, pairs_hbm, occ_hbm, tiles_ref, out_ref, pairs, occ, held_tiles, kron, held, sems):
    count, ri_width = tiles_ref.shape[0], tiles_ref.shape[2]
    occ_batch = occ_hbm.shape[0]
    width = AO_GROUP * QB
    pairs_copy = pltpu.make_async_copy(pairs_hbm, pairs, sems.at[count + 1])
    occ_copy = pltpu.make_async_copy(occ_hbm, occ, sems.at[count + 2])
    pairs_copy.start()
    occ_copy.start()
    parts = [(t, 0, AO_GROUP) for t in range(count - 1)]
    parts += [(count - 1, 0, AO_GROUP // 2), (count - 1, AO_GROUP // 2, AO_GROUP // 2)]
    copies = []
    for n, (t, r, size) in enumerate(parts):
        source, target = tiles_ref.at[t, pl.ds(r, size)], held_tiles.at[t, pl.ds(r, size)]
        copies.append(pltpu.make_async_copy(source, target, sems.at[n]))
        copies[-1].start()
    row = lax.broadcasted_iota(jnp.int32, (LANES, width), 0)
    lane = lax.broadcasted_iota(jnp.int32, (LANES, width), 1)
    spread = jnp.where(jnp.right_shift(lane, QB.bit_length() - 1) == row, 1.0, 0.0).astype(jnp.bfloat16)
    q_row = lax.broadcasted_iota(jnp.int32, (QB, width), 0)
    q_col = jnp.bitwise_and(lax.broadcasted_iota(jnp.int32, (QB, width), 1), QB - 1)
    diagonal = q_row == q_col
    pairs_copy.wait()
    occ_copy.wait()
    first = me[0] * count
    coef = [occupied_rows(occ, pairs[0, first + t] * AO_GROUP) for t in range(count)]
    coef = jnp.concatenate(coef, 0).astype(jnp.bfloat16)
    wide = jnp.dot(coef, spread, preferred_element_type=jnp.float32)
    for t in range(count):
        for i in range(occ_batch):
            rows = jnp.broadcast_to(wide[t * occ_batch + i : t * occ_batch + i + 1], (QB, width))
            kron[t, i * QB : (i + 1) * QB, :] = jnp.where(diagonal, rows, 0.0).astype(jnp.bfloat16)
    rows = occ_batch * ri_width
    for copy, (t, r, size) in zip(copies, parts):
        copy.wait()
        for b in range(0, ri_width // QB, PAIR):
            sides = [
                held_tiles[t, r : r + size, (b + k) * QB : (b + k + 1) * QB, :].reshape(size * QB, LANES)
                for k in range(PAIR)
            ]
            factor = kron[t, :, r * QB : (r + size) * QB]
            half = jnp.dot(factor, jnp.concatenate(sides, 1), preferred_element_type=jnp.float32)
            for k in range(PAIR):
                part = half[:, k * LANES : (k + 1) * LANES].reshape(occ_batch, QB, LANES)
                at = slice((b + k) * QB, (b + k + 1) * QB)
                if r > 0:
                    part = part + held[t, :, at, :]
                held[t, :, at, :] = part
    lane = lax.broadcasted_iota(jnp.int32, (rows, LANES), 1)
    pieces = []
    for s in range(count):
        tile = jnp.int32(0)
        for j in range(1, count):
            tile = jnp.where(lax.rem(pairs[1, first + j], count) == s, j, tile)
        pieces.append(held[tile].reshape(rows, LANES))
    for out in range(count * AO_GROUP // LANES):
        value = None
        for s in range(count):
            begin, end = s * AO_GROUP - out * LANES, (s + 1) * AO_GROUP - out * LANES
            if end <= 0 or begin >= LANES:
                continue
            turned = pieces[s] if begin % LANES == 0 else pltpu.roll(pieces[s], begin % LANES, 1)
            value = turned if value is None else jnp.where(lane < begin, value, turned)
        out_ref[:, out * LANES : (out + 1) * LANES] = value.astype(out_ref.dtype)


def half_transform(me, pairs, occ, tiles):
    count, ri_width = tiles.shape[0], tiles.shape[2]
    occ_batch = occ.shape[0]
    width = AO_GROUP * QB
    rows, columns = occ_batch * ri_width, count * AO_GROUP
    pairs, occ, tiles = (pltpu.with_memory_space_constraint(x, pltpu.HBM) for x in (pairs, occ, tiles))
    return pl.pallas_call(
        half_kernel,
        in_specs=[pl.BlockSpec(memory_space=pltpu.SMEM)] + [pl.BlockSpec(memory_space=pl.ANY)] * 3,
        out_specs=pl.BlockSpec(memory_space=pltpu.VMEM),
        out_shape=pltpu.VMEM((rows, columns), jnp.bfloat16),
        scratch_shapes=[
            pltpu.SMEM(pairs.shape, jnp.int32),
            pltpu.VMEM(occ.shape, jnp.bfloat16),
            pltpu.VMEM((count, AO_GROUP, ri_width, LANES), jnp.bfloat16),
            pltpu.VMEM((count, occ_batch * QB, width), jnp.bfloat16),
            pltpu.VMEM((count, occ_batch, ri_width, LANES), jnp.float32),
            pltpu.SemaphoreType.DMA((count + 3,)),
        ],
        compiler_params=pltpu.CompilerParams(vmem_limit_bytes=HALF_VMEM),
        cost_estimate=pl.CostEstimate(
            flops=2 * rows * columns * width, bytes_accessed=2 * tiles.size, transcendentals=0
        ),
        name="half_transform",
    )(me, pairs, occ, tiles)


def chip_at(place, chips):
    place = lax.rem(place + chips, chips)
    return jnp.where(place < chips // 2, 2 * place, 2 * (chips - 1 - place) + 1)


def place_of(chip, chips):
    return jnp.where(lax.rem(chip, 2) == 0, chip // 2, chips - 1 - chip // 2)


def take_windows(count, pairs, vir_ref, dev, write):
    columns = count * AO_GROUP
    panels = vir_ref.shape[1] // columns
    cols = [pairs[1, dev * count + j] for j in range(count)]
    first = cols[0]
    for col in cols:
        before = lax.rem(col + (NGROUP - 1), NGROUP)
        is_first = functools.reduce(jnp.logical_and, [other != before for other in cols])
        first = jnp.where(is_first, col, first)
    panel = first // count
    bound = lax.rem(first, count) * AO_GROUP
    low = pl.multiple_of(panel * columns, LANES)
    high = pl.multiple_of(lax.rem(panel + 1, panels) * columns, LANES)
    for j in range(columns // LANES):
        lane = lax.broadcasted_iota(jnp.int32, (QB, LANES), 1) + j * LANES
        keep = jnp.where(lane >= bound, 1.0, 0.0)
        here = vir_ref[:, pl.ds(pl.multiple_of(low + j * LANES, LANES), LANES)]
        there = vir_ref[:, pl.ds(pl.multiple_of(high + j * LANES, LANES), LANES)]
        keep, drop = keep[:1].astype(jnp.bfloat16), (1.0 - keep[:1]).astype(jnp.bfloat16)
        write(j, here * keep + there * drop)


def window_kernel(count, chips, me, pairs, vir_ref, own_ref, other_ref, last_ref):
    chip, core = me[0] // 2, lax.rem(me[0], 2)
    place = place_of(chip, chips)
    columns = count * AO_GROUP

    def store(out_ref, k, dev):
        def write(j, value):
            at = k * columns + j * LANES
            out_ref[:, at : at + LANES] = value

        take_windows(count, pairs, vir_ref, dev, write)

    for k in range(chips - 1):
        for out_ref, which in ((own_ref, core), (other_ref, 1 - core)):
            source = chip_at(place + (2 * which - 1) * ((k + 1) // 2), chips)
            store(out_ref, k, 2 * source + (which if k == 0 or k % 2 == 1 else 1 - which))
    source = chip_at(place + chips // 2, chips)
    store(last_ref, 0, 2 * source + core)
    store(last_ref, 1, 2 * source + 1 - core)


def windows(me, pairs, vir, count, chips):
    rows, columns = vir.shape[0], count * AO_GROUP
    smem, vmem = pl.BlockSpec(memory_space=pltpu.SMEM), pl.BlockSpec(memory_space=pltpu.VMEM)
    return pl.pallas_call(
        functools.partial(window_kernel, count, chips),
        in_specs=[smem, smem, vmem],
        out_specs=[vmem, vmem, vmem],
        out_shape=[
            jax.ShapeDtypeStruct((rows, (chips - 1) * columns), vir.dtype),
            jax.ShapeDtypeStruct((rows, (chips - 1) * columns), vir.dtype),
            jax.ShapeDtypeStruct((rows, 2 * columns), vir.dtype),
        ],
        compiler_params=pltpu.CompilerParams(vmem_limit_bytes=STEP_VMEM),
        cost_estimate=UNTIMED,
        name="vir_windows",
    )(me, pairs, vir)


def dot_columns(vir, block):
    return lax.dot_general(vir, block, (((1,), (1,)), ((), ())), preferred_element_type=jnp.float32)


def add_kernel(k, own_w, other_w, block, other_block, *refs):
    columns = block.shape[1]
    at = slice(k * columns, (k + 1) * columns)
    total = dot_columns(own_w[:, at], block[...]) + dot_columns(other_w[:, at], other_block[...])
    refs[-1][...] = total + refs[0][...] if len(refs) == 2 else total


def add_blocks(total, k, own_w, other_w, block, other_block):
    shape = jax.ShapeDtypeStruct((own_w.shape[0], block.shape[0]), jnp.float32)
    vmem = pl.BlockSpec(memory_space=pltpu.VMEM)
    before = () if total is None else (total,)
    return pl.pallas_call(
        functools.partial(add_kernel, k),
        in_specs=[vmem] * (4 + len(before)),
        out_specs=vmem,
        out_shape=shape,
        input_output_aliases={4: 0} if before else {},
        compiler_params=pltpu.CompilerParams(vmem_limit_bytes=STEP_VMEM),
        cost_estimate=UNTIMED,
        name="add_blocks",
    )(own_w, other_w, block, other_block, *before)


def last_kernel(last_w, last_a, last_b, other_a, before, done_ref, rest_ref):
    rows, columns = last_a.shape
    own = last_w[:, :columns]
    first = before[:, :rows] + dot_columns(own, last_a[...])
    done_ref[...] = (first + dot_columns(last_w[:, columns:], other_a[...])).astype(done_ref.dtype)
    rest_ref[...] = before[:, rows:] + dot_columns(own, last_b[...])


def add_last(last_w, last_a, last_b, other_a, before):
    vmem = pl.BlockSpec(memory_space=pltpu.VMEM)
    rows = before.shape[0]
    return pl.pallas_call(
        last_kernel,
        in_specs=[vmem] * 5,
        out_specs=[vmem] * 2,
        out_shape=[
            jax.ShapeDtypeStruct((rows, last_a.shape[0]), jnp.bfloat16),
            jax.ShapeDtypeStruct((rows, last_b.shape[0]), before.dtype),
        ],
        compiler_params=pltpu.CompilerParams(vmem_limit_bytes=STEP_VMEM),
        cost_estimate=UNTIMED,
        name="add_last",
    )(last_w, last_a, last_b, other_a, before)


def finish_kernel(last_w, block, done, rest, out_hbm, out, sems):
    columns = block.shape[1]
    split = done.shape[1]
    first = pltpu.make_async_copy(done, out_hbm.at[:, :split], sems.at[0])
    first.start()
    value = rest[...] + dot_columns(last_w[:, columns:], block[...])
    out[...] = value.astype(out.dtype)
    second = pltpu.make_async_copy(out, out_hbm.at[:, split:], sems.at[1])
    second.start()
    first.wait()
    second.wait()


def finish(last_w, block, done, rest):
    vmem = pl.BlockSpec(memory_space=pltpu.VMEM)
    return pl.pallas_call(
        finish_kernel,
        in_specs=[vmem] * 4,
        out_specs=pl.BlockSpec(memory_space=pl.ANY),
        out_shape=jax.ShapeDtypeStruct((rest.shape[0], done.shape[1] + rest.shape[1]), jnp.bfloat16),
        scratch_shapes=[pltpu.VMEM(rest.shape, jnp.bfloat16), pltpu.SemaphoreType.DMA((2,))],
        compiler_params=pltpu.CompilerParams(vmem_limit_bytes=STEP_VMEM),
        cost_estimate=UNTIMED,
        name="finish",
    )(last_w, block, done, rest)


def on_device(chips, tiles, pairs, occ_coef, vir_coef):
    count = tiles.shape[0]
    columns = count * AO_GROUP
    me = lax.axis_index("ao").astype(jnp.int32).reshape(1)
    pairs, occ, vir = pairs.T, occ_coef.T, vir_coef.T

    ring = [2 * p if p < chips // 2 else 2 * (chips - 1 - p) + 1 for p in range(chips)]
    links = [(ring[p], ring[(p + 1) % chips]) for p in range(chips)]
    onward = [(2 * a, 2 * b) for a, b in links] + [(2 * b + 1, 2 * a + 1) for a, b in links]
    across = [(d, d ^ 1) for d in range(2 * chips)]

    own = half_transform(me, pairs, occ, tiles)
    blocks, other_blocks = [own], [lax.ppermute(own, "ao", across)]
    first_other, vir = lax.optimization_barrier((other_blocks[0], vir))
    own_w, other_w, last_w = windows(me, pairs, vir, count, chips)
    total, summed = None, 0
    for message in range(1, chips):
        if message == 1:
            block = own
        elif message == 2:
            block = first_other
        else:
            block = blocks[message - 2]
        if message == 3:
            block, own_w, other_w, last_w = lax.optimization_barrier((block, own_w, other_w, last_w))
        if message > 3:
            total = add_blocks(total, summed, own_w, other_w, blocks[summed], other_blocks[summed])
            summed += 1
            if message == chips - 1:
                block, total, other_blocks[summed] = lax.optimization_barrier((block, total, other_blocks[summed]))
            else:
                block, total = lax.optimization_barrier((block, total))
        if message < chips - 1:
            block = lax.ppermute(block, "ao", onward)
            blocks.append(block)
            if message < chips - 2:
                other_blocks.append(lax.ppermute(block, "ao", across))
            else:
                h = block.shape[0] // 2
                other_blocks.append(jnp.concatenate([lax.ppermute(p, "ao", across) for p in (block[:h], block[h:])], 0))
        else:
            half = block.shape[0] // 2
            last_a = lax.ppermute(block[:half], "ao", onward)
            last_b = lax.ppermute(block[half:], "ao", onward)
    while summed < len(blocks) - 1:
        total = add_blocks(total, summed, own_w, other_w, blocks[summed], other_blocks[summed])
        summed += 1
    last_a, total = lax.optimization_barrier((last_a, total))
    other_a = lax.ppermute(last_a, "ao", across)
    last_b, total = lax.optimization_barrier((last_b, total))
    other_b = lax.ppermute(last_b, "ao", across)
    while summed < len(blocks):
        total = add_blocks(total, summed, own_w, other_w, blocks[summed], other_blocks[summed])
        summed += 1
    return finish(last_w, other_b, *add_last(last_w, last_a, last_b, other_a, total))


def solution(mesh):
    return jax.shard_map(
        functools.partial(on_device, mesh.shape["ao"] // 2),
        mesh=mesh,
        in_specs=(P("ao", None, "groups", None), P(), P(), P(None, "ao")),
        out_specs=P("ao", "groups"),
        check_vma=False,
    )
```

```python
import functools

import jax
import jax.numpy as jnp
from jax import lax
from jax.experimental import pallas as pl
from jax.experimental.pallas import tpu as pltpu
from jax.sharding import PartitionSpec as P

NGROUP = 64
AO_GROUP = 96
LANES = 128
QB = 16
PAIR = 2
HALF_VMEM = 24 * 1024 * 1024
STEP_VMEM = 24 * 1024 * 1024
UNTIMED = pl.CostEstimate(flops=0, bytes_accessed=0, transcendentals=0)


def occupied_rows(occ_ref, offset):
    start = pl.multiple_of((offset // LANES) * LANES, LANES)
    after = pl.multiple_of(jnp.minimum(start + LANES, occ_ref.shape[1] - LANES), LANES)
    shift = offset - start
    turn = lax.rem(LANES - shift, LANES)
    low = pltpu.roll(occ_ref[:, pl.ds(start, LANES)].astype(jnp.float32), turn, 1)
    high = pltpu.roll(occ_ref[:, pl.ds(after, LANES)].astype(jnp.float32), turn, 1)
    lane = lax.broadcasted_iota(jnp.int32, low.shape, 1)
    return jnp.where(lane < LANES - shift, low, high)


def half_kernel(me, pairs_hbm, occ_hbm, tiles_ref, out_ref, pairs, occ, held_tiles, kron, held, sems):
    count, ri_width = tiles_ref.shape[0], tiles_ref.shape[2]
    occ_batch = occ_hbm.shape[0]
    width = AO_GROUP * QB
    pairs_copy = pltpu.make_async_copy(pairs_hbm, pairs, sems.at[count + 1])
    occ_copy = pltpu.make_async_copy(occ_hbm, occ, sems.at[count + 2])
    pairs_copy.start()
    occ_copy.start()
    parts = [(t, 0, AO_GROUP) for t in range(count - 1)]
    parts += [(count - 1, 0, AO_GROUP // 2), (count - 1, AO_GROUP // 2, AO_GROUP // 2)]
    copies = []
    for n, (t, r, size) in enumerate(parts):
        source, target = tiles_ref.at[t, pl.ds(r, size)], held_tiles.at[t, pl.ds(r, size)]
        copies.append(pltpu.make_async_copy(source, target, sems.at[n]))
        copies[-1].start()
    row = lax.broadcasted_iota(jnp.int32, (LANES, width), 0)
    lane = lax.broadcasted_iota(jnp.int32, (LANES, width), 1)
    spread = jnp.where(jnp.right_shift(lane, QB.bit_length() - 1) == row, 1.0, 0.0).astype(jnp.bfloat16)
    q_row = lax.broadcasted_iota(jnp.int32, (QB, width), 0)
    q_col = jnp.bitwise_and(lax.broadcasted_iota(jnp.int32, (QB, width), 1), QB - 1)
    diagonal = q_row == q_col
    pairs_copy.wait()
    occ_copy.wait()
    first = me[0] * count
    coef = [occupied_rows(occ, pairs[0, first + t] * AO_GROUP) for t in range(count)]
    coef = jnp.concatenate(coef, 0).astype(jnp.bfloat16)
    wide = jnp.dot(coef, spread, preferred_element_type=jnp.float32)
    for t in range(count):
        for i in range(occ_batch):
            rows = jnp.broadcast_to(wide[t * occ_batch + i : t * occ_batch + i + 1], (QB, width))
            kron[t, i * QB : (i + 1) * QB, :] = jnp.where(diagonal, rows, 0.0).astype(jnp.bfloat16)
    rows = occ_batch * ri_width
    for copy, (t, r, size) in zip(copies, parts):
        copy.wait()
        for b in range(0, ri_width // QB, PAIR):
            sides = [
                held_tiles[t, r : r + size, (b + k) * QB : (b + k + 1) * QB, :].reshape(size * QB, LANES)
                for k in range(PAIR)
            ]
            factor = kron[t, :, r * QB : (r + size) * QB]
            half = jnp.dot(factor, jnp.concatenate(sides, 1), preferred_element_type=jnp.float32)
            for k in range(PAIR):
                part = half[:, k * LANES : (k + 1) * LANES].reshape(occ_batch, QB, LANES)
                at = slice((b + k) * QB, (b + k + 1) * QB)
                if r > 0:
                    part = part + held[t, :, at, :]
                held[t, :, at, :] = part
    lane = lax.broadcasted_iota(jnp.int32, (rows, LANES), 1)
    pieces = []
    for s in range(count):
        tile = jnp.int32(0)
        for j in range(1, count):
            tile = jnp.where(lax.rem(pairs[1, first + j], count) == s, j, tile)
        pieces.append(held[tile].reshape(rows, LANES))
    for out in range(count * AO_GROUP // LANES):
        value = None
        for s in range(count):
            begin, end = s * AO_GROUP - out * LANES, (s + 1) * AO_GROUP - out * LANES
            if end <= 0 or begin >= LANES:
                continue
            turned = pieces[s] if begin % LANES == 0 else pltpu.roll(pieces[s], begin % LANES, 1)
            value = turned if value is None else jnp.where(lane < begin, value, turned)
        out_ref[:, out * LANES : (out + 1) * LANES] = value.astype(out_ref.dtype)


def half_transform(me, pairs, occ, tiles):
    count, ri_width = tiles.shape[0], tiles.shape[2]
    occ_batch = occ.shape[0]
    width = AO_GROUP * QB
    rows, columns = occ_batch * ri_width, count * AO_GROUP
    pairs, occ, tiles = (pltpu.with_memory_space_constraint(x, pltpu.HBM) for x in (pairs, occ, tiles))
    return pl.pallas_call(
        half_kernel,
        in_specs=[pl.BlockSpec(memory_space=pltpu.SMEM)] + [pl.BlockSpec(memory_space=pl.ANY)] * 3,
        out_specs=pl.BlockSpec(memory_space=pltpu.VMEM),
        out_shape=pltpu.VMEM((rows, columns), jnp.bfloat16),
        scratch_shapes=[
            pltpu.SMEM(pairs.shape, jnp.int32),
            pltpu.VMEM(occ.shape, jnp.bfloat16),
            pltpu.VMEM((count, AO_GROUP, ri_width, LANES), jnp.bfloat16),
            pltpu.VMEM((count, occ_batch * QB, width), jnp.bfloat16),
            pltpu.VMEM((count, occ_batch, ri_width, LANES), jnp.float32),
            pltpu.SemaphoreType.DMA((count + 3,)),
        ],
        compiler_params=pltpu.CompilerParams(vmem_limit_bytes=HALF_VMEM),
        cost_estimate=pl.CostEstimate(
            flops=2 * rows * columns * width, bytes_accessed=2 * tiles.size, transcendentals=0
        ),
        name="half_transform",
    )(me, pairs, occ, tiles)


def chip_at(place, chips):
    place = lax.rem(place + chips, chips)
    return jnp.where(place < chips // 2, 2 * place, 2 * (chips - 1 - place) + 1)


def place_of(chip, chips):
    return jnp.where(lax.rem(chip, 2) == 0, chip // 2, chips - 1 - chip // 2)


def take_windows(count, pairs, vir_ref, dev, write):
    columns = count * AO_GROUP
    panels = vir_ref.shape[1] // columns
    cols = [pairs[1, dev * count + j] for j in range(count)]
    first = cols[0]
    for col in cols:
        before = lax.rem(col + (NGROUP - 1), NGROUP)
        is_first = functools.reduce(jnp.logical_and, [other != before for other in cols])
        first = jnp.where(is_first, col, first)
    panel = first // count
    bound = lax.rem(first, count) * AO_GROUP
    low = pl.multiple_of(panel * columns, LANES)
    high = pl.multiple_of(lax.rem(panel + 1, panels) * columns, LANES)
    for j in range(columns // LANES):
        lane = lax.broadcasted_iota(jnp.int32, (QB, LANES), 1) + j * LANES
        keep = jnp.where(lane >= bound, 1.0, 0.0)
        here = vir_ref[:, pl.ds(pl.multiple_of(low + j * LANES, LANES), LANES)]
        there = vir_ref[:, pl.ds(pl.multiple_of(high + j * LANES, LANES), LANES)]
        keep, drop = keep[:1].astype(jnp.bfloat16), (1.0 - keep[:1]).astype(jnp.bfloat16)
        write(j, here * keep + there * drop)


def window_kernel(count, chips, me, pairs, vir_ref, own_ref, other_ref, last_ref):
    chip, core = me[0] // 2, lax.rem(me[0], 2)
    place = place_of(chip, chips)
    columns = count * AO_GROUP

    def store(out_ref, k, dev):
        def write(j, value):
            at = k * columns + j * LANES
            out_ref[:, at : at + LANES] = value

        take_windows(count, pairs, vir_ref, dev, write)

    for k in range(chips - 1):
        for out_ref, which in ((own_ref, core), (other_ref, 1 - core)):
            source = chip_at(place + (2 * which - 1) * ((k + 1) // 2), chips)
            store(out_ref, k, 2 * source + (which if k == 0 or k % 2 == 1 else 1 - which))
    source = chip_at(place + chips // 2, chips)
    store(last_ref, 0, 2 * source + core)
    store(last_ref, 1, 2 * source + 1 - core)


def windows(me, pairs, vir, count, chips):
    rows, columns = vir.shape[0], count * AO_GROUP
    smem, vmem = pl.BlockSpec(memory_space=pltpu.SMEM), pl.BlockSpec(memory_space=pltpu.VMEM)
    return pl.pallas_call(
        functools.partial(window_kernel, count, chips),
        in_specs=[smem, smem, vmem],
        out_specs=[vmem, vmem, vmem],
        out_shape=[
            jax.ShapeDtypeStruct((rows, (chips - 1) * columns), vir.dtype),
            jax.ShapeDtypeStruct((rows, (chips - 1) * columns), vir.dtype),
            jax.ShapeDtypeStruct((rows, 2 * columns), vir.dtype),
        ],
        compiler_params=pltpu.CompilerParams(vmem_limit_bytes=STEP_VMEM),
        cost_estimate=UNTIMED,
        name="vir_windows",
    )(me, pairs, vir)


def dot_columns(vir, block):
    return lax.dot_general(vir, block, (((1,), (1,)), ((), ())), preferred_element_type=jnp.float32)


def add_kernel(k, own_w, other_w, block, other_block, *refs):
    columns = block.shape[1]
    at = slice(k * columns, (k + 1) * columns)
    total = dot_columns(own_w[:, at], block[...]) + dot_columns(other_w[:, at], other_block[...])
    refs[-1][...] = total + refs[0][...] if len(refs) == 2 else total


def add_blocks(total, k, own_w, other_w, block, other_block):
    shape = jax.ShapeDtypeStruct((own_w.shape[0], block.shape[0]), jnp.float32)
    vmem = pl.BlockSpec(memory_space=pltpu.VMEM)
    before = () if total is None else (total,)
    return pl.pallas_call(
        functools.partial(add_kernel, k),
        in_specs=[vmem] * (4 + len(before)),
        out_specs=vmem,
        out_shape=shape,
        input_output_aliases={4: 0} if before else {},
        compiler_params=pltpu.CompilerParams(vmem_limit_bytes=STEP_VMEM),
        cost_estimate=UNTIMED,
        name="add_blocks",
    )(own_w, other_w, block, other_block, *before)


def last_kernel(last_w, last_a, last_b, other_a, before, done_ref, rest_ref):
    rows, columns = last_a.shape
    own = last_w[:, :columns]
    first = before[:, :rows] + dot_columns(own, last_a[...])
    done_ref[...] = (first + dot_columns(last_w[:, columns:], other_a[...])).astype(done_ref.dtype)
    rest_ref[...] = before[:, rows:] + dot_columns(own, last_b[...])


def add_last(last_w, last_a, last_b, other_a, before):
    vmem = pl.BlockSpec(memory_space=pltpu.VMEM)
    rows = before.shape[0]
    return pl.pallas_call(
        last_kernel,
        in_specs=[vmem] * 5,
        out_specs=[vmem] * 2,
        out_shape=[
            jax.ShapeDtypeStruct((rows, last_a.shape[0]), jnp.bfloat16),
            jax.ShapeDtypeStruct((rows, last_b.shape[0]), before.dtype),
        ],
        compiler_params=pltpu.CompilerParams(vmem_limit_bytes=STEP_VMEM),
        cost_estimate=UNTIMED,
        name="add_last",
    )(last_w, last_a, last_b, other_a, before)


def finish_kernel(last_w, block, done, rest, out_hbm, out, sems):
    columns = block.shape[1]
    split = done.shape[1]
    first = pltpu.make_async_copy(done, out_hbm.at[:, :split], sems.at[0])
    first.start()
    value = rest[...] + dot_columns(last_w[:, columns:], block[...])
    out[...] = value.astype(out.dtype)
    second = pltpu.make_async_copy(out, out_hbm.at[:, split:], sems.at[1])
    second.start()
    first.wait()
    second.wait()


def finish(last_w, block, done, rest):
    vmem = pl.BlockSpec(memory_space=pltpu.VMEM)
    return pl.pallas_call(
        finish_kernel,
        in_specs=[vmem] * 4,
        out_specs=pl.BlockSpec(memory_space=pl.ANY),
        out_shape=jax.ShapeDtypeStruct((rest.shape[0], done.shape[1] + rest.shape[1]), jnp.bfloat16),
        scratch_shapes=[pltpu.VMEM(rest.shape, jnp.bfloat16), pltpu.SemaphoreType.DMA((2,))],
        compiler_params=pltpu.CompilerParams(vmem_limit_bytes=STEP_VMEM),
        cost_estimate=UNTIMED,
        name="finish",
    )(last_w, block, done, rest)


def on_device(chips, tiles, pairs, occ_coef, vir_coef):
    count = tiles.shape[0]
    columns = count * AO_GROUP
    me = lax.axis_index("ao").astype(jnp.int32).reshape(1)
    pairs, occ, vir = pairs.T, occ_coef.T, vir_coef.T

    ring = [2 * p if p < chips // 2 else 2 * (chips - 1 - p) + 1 for p in range(chips)]
    links = [(ring[p], ring[(p + 1) % chips]) for p in range(chips)]
    onward = [(2 * a, 2 * b) for a, b in links] + [(2 * b + 1, 2 * a + 1) for a, b in links]
    across = [(d, d ^ 1) for d in range(2 * chips)]

    own = half_transform(me, pairs, occ, tiles)
    blocks, other_blocks = [own], [lax.ppermute(own, "ao", across)]
    first_other = other_blocks[0]
    own_w, other_w, last_w = windows(me, pairs, vir, count, chips)
    total, summed = None, 0
    for message in range(1, chips):
        if message == 1:
            block = own
        elif message == 2:
            block = first_other
        else:
            block = blocks[message - 2]
        if message == 3:
            block, own_w, other_w, last_w = lax.optimization_barrier((block, own_w, other_w, last_w))
        if message > 3:
            total = add_blocks(total, summed, own_w, other_w, blocks[summed], other_blocks[summed])
            summed += 1
            if message == chips - 1:
                block, total, other_blocks[summed] = lax.optimization_barrier((block, total, other_blocks[summed]))
            else:
                block, total = lax.optimization_barrier((block, total))
        if message < chips - 1:
            block = lax.ppermute(block, "ao", onward)
            blocks.append(block)
            if message < chips - 2:
                other_blocks.append(lax.ppermute(block, "ao", across))
            else:
                h = block.shape[0] // 2
                other_blocks.append(jnp.concatenate([lax.ppermute(p, "ao", across) for p in (block[:h], block[h:])], 0))
        else:
            half = block.shape[0] // 2
            last_a = lax.ppermute(block[:half], "ao", onward)
            last_b = lax.ppermute(block[half:], "ao", onward)
    while summed < len(blocks) - 1:
        total = add_blocks(total, summed, own_w, other_w, blocks[summed], other_blocks[summed])
        summed += 1
    last_a, total = lax.optimization_barrier((last_a, total))
    other_a = lax.ppermute(last_a, "ao", across)
    last_b, total = lax.optimization_barrier((last_b, total))
    other_b = lax.ppermute(last_b, "ao", across)
    while summed < len(blocks):
        total = add_blocks(total, summed, own_w, other_w, blocks[summed], other_blocks[summed])
        summed += 1
    return finish(last_w, other_b, *add_last(last_w, last_a, last_b, other_a, total))


def solution(mesh):
    return jax.shard_map(
        functools.partial(on_device, mesh.shape["ao"] // 2),
        mesh=mesh,
        in_specs=(P("ao", None, "groups", None), P(), P(), P(None, "ao")),
        out_specs=P("ao", "groups"),
        check_vma=False,
    )
```

```python
import functools

import jax
import jax.numpy as jnp
from jax import lax
from jax.experimental import pallas as pl
from jax.experimental.pallas import tpu as pltpu
from jax.sharding import PartitionSpec as P

NGROUP = 64
AO_GROUP = 96
LANES = 128
QB = 16
PAIR = 2
HALF_VMEM = 24 * 1024 * 1024
STEP_VMEM = 24 * 1024 * 1024
UNTIMED = pl.CostEstimate(flops=0, bytes_accessed=0, transcendentals=0)


def occupied_rows(occ_ref, offset):
    start = pl.multiple_of((offset // LANES) * LANES, LANES)
    after = pl.multiple_of(jnp.minimum(start + LANES, occ_ref.shape[1] - LANES), LANES)
    shift = offset - start
    turn = lax.rem(LANES - shift, LANES)
    low = pltpu.roll(occ_ref[:, pl.ds(start, LANES)].astype(jnp.float32), turn, 1)
    high = pltpu.roll(occ_ref[:, pl.ds(after, LANES)].astype(jnp.float32), turn, 1)
    lane = lax.broadcasted_iota(jnp.int32, low.shape, 1)
    return jnp.where(lane < LANES - shift, low, high)


def half_kernel(me, pairs_hbm, occ_hbm, tiles_ref, out_ref, pairs, occ, held_tiles, kron, held, sems):
    count, ri_width = tiles_ref.shape[0], tiles_ref.shape[2]
    occ_batch = occ_hbm.shape[0]
    width = AO_GROUP * QB
    pairs_copy = pltpu.make_async_copy(pairs_hbm, pairs, sems.at[count + 1])
    occ_copy = pltpu.make_async_copy(occ_hbm, occ, sems.at[count + 2])
    pairs_copy.start()
    occ_copy.start()
    parts = [(t, 0, AO_GROUP) for t in range(count - 1)]
    parts += [(count - 1, 0, AO_GROUP // 2), (count - 1, AO_GROUP // 2, AO_GROUP // 2)]
    copies = []
    for n, (t, r, size) in enumerate(parts):
        source, target = tiles_ref.at[t, pl.ds(r, size)], held_tiles.at[t, pl.ds(r, size)]
        copies.append(pltpu.make_async_copy(source, target, sems.at[n]))
        copies[-1].start()
    row = lax.broadcasted_iota(jnp.int32, (LANES, width), 0)
    lane = lax.broadcasted_iota(jnp.int32, (LANES, width), 1)
    spread = jnp.where(jnp.right_shift(lane, QB.bit_length() - 1) == row, 1.0, 0.0).astype(jnp.bfloat16)
    q_row = lax.broadcasted_iota(jnp.int32, (QB, width), 0)
    q_col = jnp.bitwise_and(lax.broadcasted_iota(jnp.int32, (QB, width), 1), QB - 1)
    diagonal = q_row == q_col
    pairs_copy.wait()
    occ_copy.wait()
    first = me[0] * count
    coef = [occupied_rows(occ, pairs[0, first + t] * AO_GROUP) for t in range(count)]
    coef = jnp.concatenate(coef, 0).astype(jnp.bfloat16)
    wide = jnp.dot(coef, spread, preferred_element_type=jnp.float32)
    for t in range(count):
        for i in range(occ_batch):
            rows = jnp.broadcast_to(wide[t * occ_batch + i : t * occ_batch + i + 1], (QB, width))
            kron[t, i * QB : (i + 1) * QB, :] = jnp.where(diagonal, rows, 0.0).astype(jnp.bfloat16)
    rows = occ_batch * ri_width
    for copy, (t, r, size) in zip(copies, parts):
        copy.wait()
        for b in range(0, ri_width // QB, PAIR):
            sides = [
                held_tiles[t, r : r + size, (b + k) * QB : (b + k + 1) * QB, :].reshape(size * QB, LANES)
                for k in range(PAIR)
            ]
            factor = kron[t, :, r * QB : (r + size) * QB]
            half = jnp.dot(factor, jnp.concatenate(sides, 1), preferred_element_type=jnp.float32)
            for k in range(PAIR):
                part = half[:, k * LANES : (k + 1) * LANES].reshape(occ_batch, QB, LANES)
                at = slice((b + k) * QB, (b + k + 1) * QB)
                if r > 0:
                    part = part + held[t, :, at, :]
                held[t, :, at, :] = part
    lane = lax.broadcasted_iota(jnp.int32, (rows, LANES), 1)
    pieces = []
    for s in range(count):
        tile = jnp.int32(0)
        for j in range(1, count):
            tile = jnp.where(lax.rem(pairs[1, first + j], count) == s, j, tile)
        pieces.append(held[tile].reshape(rows, LANES))
    for out in range(count * AO_GROUP // LANES):
        value = None
        for s in range(count):
            begin, end = s * AO_GROUP - out * LANES, (s + 1) * AO_GROUP - out * LANES
            if end <= 0 or begin >= LANES:
                continue
            turned = pieces[s] if begin % LANES == 0 else pltpu.roll(pieces[s], begin % LANES, 1)
            value = turned if value is None else jnp.where(lane < begin, value, turned)
        out_ref[:, out * LANES : (out + 1) * LANES] = value.astype(out_ref.dtype)


def half_transform(me, pairs, occ, tiles):
    count, ri_width = tiles.shape[0], tiles.shape[2]
    occ_batch = occ.shape[0]
    width = AO_GROUP * QB
    rows, columns = occ_batch * ri_width, count * AO_GROUP
    pairs, occ, tiles = (pltpu.with_memory_space_constraint(x, pltpu.HBM) for x in (pairs, occ, tiles))
    return pl.pallas_call(
        half_kernel,
        in_specs=[pl.BlockSpec(memory_space=pltpu.SMEM)] + [pl.BlockSpec(memory_space=pl.ANY)] * 3,
        out_specs=pl.BlockSpec(memory_space=pltpu.VMEM),
        out_shape=pltpu.VMEM((rows, columns), jnp.bfloat16),
        scratch_shapes=[
            pltpu.SMEM(pairs.shape, jnp.int32),
            pltpu.VMEM(occ.shape, jnp.bfloat16),
            pltpu.VMEM((count, AO_GROUP, ri_width, LANES), jnp.bfloat16),
            pltpu.VMEM((count, occ_batch * QB, width), jnp.bfloat16),
            pltpu.VMEM((count, occ_batch, ri_width, LANES), jnp.float32),
            pltpu.SemaphoreType.DMA((count + 3,)),
        ],
        compiler_params=pltpu.CompilerParams(vmem_limit_bytes=HALF_VMEM),
        cost_estimate=pl.CostEstimate(
            flops=2 * rows * columns * width, bytes_accessed=2 * tiles.size, transcendentals=0
        ),
        name="half_transform",
    )(me, pairs, occ, tiles)


def chip_at(place, chips):
    place = lax.rem(place + chips, chips)
    return jnp.where(place < chips // 2, 2 * place, 2 * (chips - 1 - place) + 1)


def place_of(chip, chips):
    return jnp.where(lax.rem(chip, 2) == 0, chip // 2, chips - 1 - chip // 2)


def take_windows(count, pairs, vir_ref, dev, write):
    columns = count * AO_GROUP
    panels = vir_ref.shape[1] // columns
    cols = [pairs[1, dev * count + j] for j in range(count)]
    first = cols[0]
    for col in cols:
        before = lax.rem(col + (NGROUP - 1), NGROUP)
        is_first = functools.reduce(jnp.logical_and, [other != before for other in cols])
        first = jnp.where(is_first, col, first)
    panel = first // count
    bound = lax.rem(first, count) * AO_GROUP
    low = pl.multiple_of(panel * columns, LANES)
    high = pl.multiple_of(lax.rem(panel + 1, panels) * columns, LANES)
    for j in range(columns // LANES):
        lane = lax.broadcasted_iota(jnp.int32, (QB, LANES), 1) + j * LANES
        keep = jnp.where(lane >= bound, 1.0, 0.0)
        here = vir_ref[:, pl.ds(pl.multiple_of(low + j * LANES, LANES), LANES)]
        there = vir_ref[:, pl.ds(pl.multiple_of(high + j * LANES, LANES), LANES)]
        keep, drop = keep[:1].astype(jnp.bfloat16), (1.0 - keep[:1]).astype(jnp.bfloat16)
        write(j, here * keep + there * drop)


def window_kernel(count, chips, me, pairs, vir_ref, own_ref, other_ref, last_ref):
    chip, core = me[0] // 2, lax.rem(me[0], 2)
    place = place_of(chip, chips)
    columns = count * AO_GROUP

    def store(out_ref, k, dev):
        def write(j, value):
            at = k * columns + j * LANES
            out_ref[:, at : at + LANES] = value

        take_windows(count, pairs, vir_ref, dev, write)

    for k in range(chips - 1):
        for out_ref, which in ((own_ref, core), (other_ref, 1 - core)):
            source = chip_at(place + (2 * which - 1) * ((k + 1) // 2), chips)
            store(out_ref, k, 2 * source + (which if k == 0 or k % 2 == 1 else 1 - which))
    source = chip_at(place + chips // 2, chips)
    store(last_ref, 0, 2 * source + core)
    store(last_ref, 1, 2 * source + 1 - core)


def windows(me, pairs, vir, count, chips):
    rows, columns = vir.shape[0], count * AO_GROUP
    smem, vmem = pl.BlockSpec(memory_space=pltpu.SMEM), pl.BlockSpec(memory_space=pltpu.VMEM)
    return pl.pallas_call(
        functools.partial(window_kernel, count, chips),
        in_specs=[smem, smem, vmem],
        out_specs=[vmem, vmem, vmem],
        out_shape=[
            jax.ShapeDtypeStruct((rows, (chips - 1) * columns), vir.dtype),
            jax.ShapeDtypeStruct((rows, (chips - 1) * columns), vir.dtype),
            jax.ShapeDtypeStruct((rows, 2 * columns), vir.dtype),
        ],
        compiler_params=pltpu.CompilerParams(vmem_limit_bytes=STEP_VMEM),
        cost_estimate=pl.CostEstimate(flops=0, bytes_accessed=4 * vir.size, transcendentals=0),
        name="vir_windows",
    )(me, pairs, vir)


def dot_columns(vir, block):
    return lax.dot_general(vir, block, (((1,), (1,)), ((), ())), preferred_element_type=jnp.float32)


def add_kernel(k, own_w, other_w, block, other_block, *refs):
    columns = block.shape[1]
    at = slice(k * columns, (k + 1) * columns)
    total = dot_columns(own_w[:, at], block[...]) + dot_columns(other_w[:, at], other_block[...])
    refs[-1][...] = total + refs[0][...] if len(refs) == 2 else total


def add_blocks(total, k, own_w, other_w, block, other_block):
    shape = jax.ShapeDtypeStruct((own_w.shape[0], block.shape[0]), jnp.float32)
    vmem = pl.BlockSpec(memory_space=pltpu.VMEM)
    before = () if total is None else (total,)
    return pl.pallas_call(
        functools.partial(add_kernel, k),
        in_specs=[vmem] * (4 + len(before)),
        out_specs=vmem,
        out_shape=shape,
        input_output_aliases={4: 0} if before else {},
        compiler_params=pltpu.CompilerParams(vmem_limit_bytes=STEP_VMEM),
        cost_estimate=UNTIMED,
        name="add_blocks",
    )(own_w, other_w, block, other_block, *before)


def last_kernel(last_w, last_a, last_b, other_a, before, done_ref, rest_ref):
    rows, columns = last_a.shape
    own = last_w[:, :columns]
    first = before[:, :rows] + dot_columns(own, last_a[...])
    done_ref[...] = (first + dot_columns(last_w[:, columns:], other_a[...])).astype(done_ref.dtype)
    rest_ref[...] = before[:, rows:] + dot_columns(own, last_b[...])


def add_last(last_w, last_a, last_b, other_a, before):
    vmem = pl.BlockSpec(memory_space=pltpu.VMEM)
    rows = before.shape[0]
    return pl.pallas_call(
        last_kernel,
        in_specs=[vmem] * 5,
        out_specs=[vmem] * 2,
        out_shape=[
            jax.ShapeDtypeStruct((rows, last_a.shape[0]), jnp.bfloat16),
            jax.ShapeDtypeStruct((rows, last_b.shape[0]), before.dtype),
        ],
        compiler_params=pltpu.CompilerParams(vmem_limit_bytes=STEP_VMEM),
        cost_estimate=UNTIMED,
        name="add_last",
    )(last_w, last_a, last_b, other_a, before)


def finish_kernel(last_w, block, done, rest, out_hbm, out, sems):
    columns = block.shape[1]
    split = done.shape[1]
    first = pltpu.make_async_copy(done, out_hbm.at[:, :split], sems.at[0])
    first.start()
    value = rest[...] + dot_columns(last_w[:, columns:], block[...])
    out[...] = value.astype(out.dtype)
    second = pltpu.make_async_copy(out, out_hbm.at[:, split:], sems.at[1])
    second.start()
    first.wait()
    second.wait()


def finish(last_w, block, done, rest):
    vmem = pl.BlockSpec(memory_space=pltpu.VMEM)
    return pl.pallas_call(
        finish_kernel,
        in_specs=[vmem] * 4,
        out_specs=pl.BlockSpec(memory_space=pl.ANY),
        out_shape=jax.ShapeDtypeStruct((rest.shape[0], done.shape[1] + rest.shape[1]), jnp.bfloat16),
        scratch_shapes=[pltpu.VMEM(rest.shape, jnp.bfloat16), pltpu.SemaphoreType.DMA((2,))],
        compiler_params=pltpu.CompilerParams(vmem_limit_bytes=STEP_VMEM),
        cost_estimate=UNTIMED,
        name="finish",
    )(last_w, block, done, rest)


def on_device(chips, tiles, pairs, occ_coef, vir_coef):
    count = tiles.shape[0]
    columns = count * AO_GROUP
    me = lax.axis_index("ao").astype(jnp.int32).reshape(1)
    pairs, occ, vir = pairs.T, occ_coef.T, vir_coef.T

    ring = [2 * p if p < chips // 2 else 2 * (chips - 1 - p) + 1 for p in range(chips)]
    links = [(ring[p], ring[(p + 1) % chips]) for p in range(chips)]
    onward = [(2 * a, 2 * b) for a, b in links] + [(2 * b + 1, 2 * a + 1) for a, b in links]
    across = [(d, d ^ 1) for d in range(2 * chips)]

    own = half_transform(me, pairs, occ, tiles)
    blocks, other_blocks = [own], [lax.ppermute(own, "ao", across)]
    first_other = other_blocks[0]
    own_w, other_w, last_w = windows(me, pairs, vir, count, chips)
    total, summed = None, 0
    for message in range(1, chips):
        if message == 1:
            block = own
        elif message == 2:
            block = first_other
        else:
            block = blocks[message - 2]
        if message == 3:
            block, own_w, other_w, last_w = lax.optimization_barrier((block, own_w, other_w, last_w))
        if message > 3:
            total = add_blocks(total, summed, own_w, other_w, blocks[summed], other_blocks[summed])
            summed += 1
            if message == chips - 1:
                block, total, other_blocks[summed] = lax.optimization_barrier((block, total, other_blocks[summed]))
            else:
                block, total = lax.optimization_barrier((block, total))
        if message < chips - 1:
            block = lax.ppermute(block, "ao", onward)
            blocks.append(block)
            if message < chips - 2:
                other_blocks.append(lax.ppermute(block, "ao", across))
            else:
                h = block.shape[0] // 2
                other_blocks.append(jnp.concatenate([lax.ppermute(p, "ao", across) for p in (block[:h], block[h:])], 0))
        else:
            half = block.shape[0] // 2
            last_a = lax.ppermute(block[:half], "ao", onward)
            last_b = lax.ppermute(block[half:], "ao", onward)
    while summed < len(blocks) - 1:
        total = add_blocks(total, summed, own_w, other_w, blocks[summed], other_blocks[summed])
        summed += 1
    last_a, total = lax.optimization_barrier((last_a, total))
    other_a = lax.ppermute(last_a, "ao", across)
    last_b, total = lax.optimization_barrier((last_b, total))
    other_b = lax.ppermute(last_b, "ao", across)
    while summed < len(blocks):
        total = add_blocks(total, summed, own_w, other_w, blocks[summed], other_blocks[summed])
        summed += 1
    return finish(last_w, other_b, *add_last(last_w, last_a, last_b, other_a, total))


def solution(mesh):
    return jax.shard_map(
        functools.partial(on_device, mesh.shape["ao"] // 2),
        mesh=mesh,
        in_specs=(P("ao", None, "groups", None), P(), P(), P(None, "ao")),
        out_specs=P("ao", "groups"),
        check_vma=False,
    )
```
